256 devices in a mesh: lat: 16 (over z, y_lo), lay: 16 (over y_hi, x, core).
Axes of the slice: x: 4, y: 4 (y_hi: 2, y_lo: 2; y = y_hi * 2 + y_lo), z: 8, core: 2. Of those that a mesh axis runs over, the one named last changes fastest.
Arguments:
- wave_field: float32 [2, 128, 512, 512], P(None, 'lay', 'lat'), may hold values from -6 to 6
- contrast: float32 [128, 512, 512], P('lay', 'lat'), may hold values from 0.1 to 1.5
- layer_of_plane: int32 [128], replicated, may hold values from 0 to 7, never falling along the last dimension, each value on 1 to 32 neighbouring positions
- toeplitz_table: float32 [2, 8, 255], replicated, may hold values from -0.5 to 0.5
- hankel_table: float32 [2, 8, 255], replicated, may hold values from -0.5 to 0.5
- layer_rates: float32 [8], replicated, may hold values from 0.5 to 1.5
Outputs:
- scattered_field: float32 [2, 128, 512, 512], P(None, 'lay', 'lat')
The draws below stay inside these ranges and needn't reach their ends.
Inputs may be any that keep to these rules, and one draw needn't show every extreme that they name: `layer_of_plane`: layer numbers never fall from one plane to the next; every layer holds 1 to 32 planes.
All inputs are finite; a program needn't handle non-finite values.
Results may differ from the reference program's by a relative error of at most 0.00007.
Values sent between devices are 32-bit elements; how exact they have to be, the bound alone decides.
No kernel may reach another device: no remote copies, remote signals or barrier semaphores. Data moves between devices by JAX's collectives and lax.ppermute only.
A program may use at most 128 MiB of HBM per device.

```python
import math
import jax
import jax.numpy as jnp
import numpy as np
from jax import lax

NX = 512
NY = 512
LAYERS = 8
NZ = 128


def steps_of(key, shape, cuts, least, largest):
    factor_of, own = 1.0, jax.random.fold_in(key, 6)
    for position, parts in cuts:
        steps = jnp.exp(jax.random.uniform(jax.random.fold_in(own, position), (parts,), jnp.float32, least / len(cuts), largest / len(cuts)))
        factor_of = factor_of * jnp.repeat(steps, shape[position] // parts).reshape([-1 if axis == position else 1 for axis in range(len(shape))])
    return factor_of


def profile(count, total, reach, skew):
    portions = [(1 << 20) // math.isqrt(rank ** skew) + 1 for rank in range(2, count + 1)]
    surplus, given = total - reach - (count - 1), [1] * (count - 1)
    while surplus > 0:
        movable = [i for i in range(count - 1) if given[i] < reach]
        mass, left = sum([portions[i] for i in movable]), surplus
        for i in movable:
            extra = min(reach - given[i], max(1, left * portions[i] // mass), surplus)
            given[i] = given[i] + extra
            surplus = surplus - extra
    return np.array([reach] + given)


def uneven_parts(own_key, number_of, total, most, slope):
    if number_of == 2:
        one = jax.random.randint(own_key, (), max(1, total - most), min(most, total - 1) + 1)
        return jnp.stack([one, total - one])
    lengths = jnp.asarray(profile(number_of, total, most, slope), jnp.int32)
    twos = (number_of - 1) // 2
    giver, taker = lengths[1:1 + 2 * twos:2], lengths[2:2 + 2 * twos:2]
    margin = jnp.minimum(giver - 1, most - taker)
    shifted = jax.random.randint(jax.random.fold_in(own_key, 1), (twos,), 0, 1 << 20) % (margin + 1)
    lengths = lengths.at[1:1 + 2 * twos:2].set(giver - shifted).at[2:2 + 2 * twos:2].set(taker + shifted)
    return lengths[jax.random.permutation(jax.random.fold_in(own_key, 2), number_of)]


def noise(key, shape, scale, reach, pieces=(), dtype=jnp.bfloat16):
    factor_of = steps_of(key, shape, pieces, -0.22, 0.18) if pieces else 1.0
    array = jax.random.normal(key, shape, jnp.float32) * scale * factor_of
    return jnp.minimum(jnp.maximum(array, -reach), reach).astype(dtype)


def setup_inputs(seed: int = 0) -> dict:
    key_list = jax.random.split(jax.random.key(seed), 7)
    wave_field = noise(key_list[0], (2, NZ, NX, NY), 1.0, 6.0, ((1, 16), (2, 16)), jnp.float32)
    contrast = jnp.clip(0.1 + 1.4 * jax.random.uniform(key_list[1], (NZ, NX, NY), jnp.float32) ** steps_of(key_list[1], (NZ, NX, NY), ((0, 16), (1, 16)), -0.2, 0.2), 0.1, 1.5)
    layer_of_plane = jnp.searchsorted(jnp.cumsum(uneven_parts(key_list[2], LAYERS, NZ, 2 * NZ // LAYERS, 2)), jnp.arange(NZ), side="right").astype(jnp.int32)
    toeplitz_table = noise(key_list[3], (2, LAYERS, 2 * NZ - 1), NZ ** -0.5, 0.5, (), jnp.float32)
    hankel_table = noise(key_list[4], (2, LAYERS, 2 * NZ - 1), NZ ** -0.5, 0.5, (), jnp.float32)
    layer_rates = jnp.clip(jnp.exp(jax.random.uniform(key_list[5], (LAYERS,), jnp.float32, math.log(0.5), math.log(1.5))), 0.5, 1.5)
    return {"wave_field": wave_field, "contrast": contrast, "layer_of_plane": layer_of_plane, "toeplitz_table": toeplitz_table, "hankel_table": hankel_table, "layer_rates": layer_rates}


def signed_freq(amount):
    index = jnp.arange(amount).astype(jnp.int32)
    return jnp.where(index >= amount // 2, index - amount, index).astype(jnp.float32) / (amount / 2)

def reference(wave_field, contrast, layer_of_plane, toeplitz_table, hankel_table, layer_rates):
    complex_field = wave_field[0] + 1j * wave_field[1]
    spectrum = jnp.fft.fft2(complex_field, axes=(1, 2))
    freq_x = signed_freq(NX)
    freq_y = signed_freq(NY)
    steepness = jnp.sqrt(1.0 + freq_x[:, None] ** 2 + freq_y[None, :] ** 2)
    planes = jnp.arange(NZ).astype(jnp.int32)
    toeplitz_c = toeplitz_table[0] + 1j * toeplitz_table[1]
    hankel_c = hankel_table[0] + 1j * hankel_table[1]

    def one_plane(plane):
        layer_here = layer_of_plane[plane]
        rate_here = layer_rates[layer_here]
        offset = plane - planes
        amp_toeplitz = toeplitz_c[layer_here, offset + NZ - 1]
        amp_hankel = hankel_c[layer_here, plane + planes]
        decay_toeplitz = jnp.exp(-rate_here * steepness[None] * jnp.abs(offset).astype(jnp.float32)[:, None, None] / NZ)
        decay_hankel = jnp.exp(-rate_here * steepness[None] * (plane + planes).astype(jnp.float32)[:, None, None] / (2 * NZ))
        kernel = amp_toeplitz[:, None, None] * decay_toeplitz + amp_hankel[:, None, None] * decay_hankel
        return lax.optimization_barrier(jnp.sum(kernel * spectrum, axis=0))
    mixed = lax.map(one_plane, planes)
    space = jnp.fft.ifft2(mixed, axes=(1, 2))
    return jnp.stack([jnp.real(space) * contrast, jnp.imag(space) * contrast]).astype(jnp.float32)
```

```python
import functools
import math

import jax
import jax.numpy as jnp
import numpy as np
import ml_dtypes
from jax import lax
from jax.experimental import pallas as pl
from jax.experimental.pallas import tpu as pltpu
from jax.sharding import PartitionSpec as P

AXES = ("lay", "lat")
F32 = jnp.float32
BF16 = jnp.bfloat16
HALF = 256
PLANES = 128
LAYERS = 8
MIB = 1 << 20


def split_np(x):
    x = x.astype(np.float32)
    hi = x.astype(ml_dtypes.bfloat16)
    lo = (x - hi.astype(np.float32)).astype(ml_dtypes.bfloat16)
    return hi, lo


def dft_tables():
    index = np.arange(HALF)
    angle = 2.0 * math.pi / HALF * ((index[:, None] * index[None, :]) % HALF)
    hi, lo = split_np(np.concatenate([np.cos(angle), np.sin(angle)], 0))
    turn = 2.0 * math.pi / (2 * HALF) * index
    return hi, lo, np.stack([np.cos(turn), np.sin(turn)]).astype(np.float32)


def split(x):
    hi = x.astype(BF16)
    return hi, (x - hi.astype(F32)).astype(BF16)


def dot_nt(a, b):
    return lax.dot_general(a, b, (((1,), (1,)), ((), ())), preferred_element_type=F32)


def dot3(a_hi, a_lo, b_hi, b_lo):
    return dot_nt(a_hi, b_hi) + dot_nt(a_hi, b_lo) + dot_nt(a_lo, b_hi)


def forward_y_kernel(w_ref, hi_ref, lo_ref, tw_ref, o_ref):
    cos, sin = tw_ref[0:1, :], tw_ref[1:2, :]
    t_hi, t_lo = hi_ref[...], lo_ref[...]
    lane = lax.broadcasted_iota(jnp.int32, (HALF, 128), 1)
    planes = w_ref.shape[1]
    for pair in range(planes // 2):
        rows = []
        for z in (2 * pair, 2 * pair + 1):
            first = [w_ref[c, z, :, :HALF] for c in (0, 1)]
            second = [w_ref[c, z, :, HALF:] for c in (0, 1)]
            even = [first[c] + second[c] for c in (0, 1)]
            odd = [first[c] - second[c] for c in (0, 1)]
            odd_re = odd[0] * cos + odd[1] * sin
            odd_im = odd[1] * cos - odd[0] * sin
            rows += [even[0], odd_re, even[1], odd_im]
        v_hi, v_lo = split(jnp.concatenate(rows, 0))
        out = dot3(t_hi, t_lo, v_hi, v_lo)
        for k in (0, 1):
            with_cos = out[:HALF, 128 * k : 128 * (k + 1)]
            with_sin = pltpu.roll(out[HALF:, 128 * k : 128 * (k + 1)], 64, 1)
            o_ref[pl.ds(2 * pair + k, HALF, stride=8), :] = with_cos + jnp.where(lane < 64, with_sin, -with_sin)


def tables_kernel(layer_ref, toe_ref, han_ref, r_ref):
    layer_rows = jnp.transpose(jnp.broadcast_to(layer_ref[...].astype(F32), (PLANES, PLANES)))
    wide = jnp.concatenate([layer_rows, layer_rows], 1)
    row = lax.broadcasted_iota(jnp.int32, (PLANES, 2 * PLANES), 0)

    def spread(ref, c, amount):
        x = jnp.zeros((PLANES, 2 * PLANES), F32)
        for l in range(LAYERS):
            x = jnp.where(wide == float(l), ref[c, l : l + 1, :], x)
        for bit in range(7):
            moved = pltpu.roll(x, 2 * PLANES - (1 << bit), 1)
            x = jnp.where(((amount >> bit) & 1) == 1, moved, x)
        return x[:, :PLANES]

    toe = [spread(toe_ref, c, PLANES - 1 - row) for c in (0, 1)]
    han = [spread(han_ref, c, row) for c in (0, 1)]
    z = lax.broadcasted_iota(jnp.int32, (PLANES, PLANES), 0)
    s = lax.broadcasted_iota(jnp.int32, (PLANES, PLANES), 1)
    low = [jnp.where(s <= z, x, 0.0) for x in toe]
    high = [jnp.where(s > z, x, 0.0) for x in toe]
    for t, (re, im) in enumerate((low, high, han)):
        for out_part, blocks in enumerate(((re, -im), (im, re))):
            for in_part, block in enumerate(blocks):
                hi = block.astype(BF16).astype(F32)
                lo = block - hi
                for l in range(LAYERS):
                    here = layer_rows == float(l)
                    rows = slice(PLANES * out_part, PLANES * (out_part + 1))
                    at = 2 * PLANES * l + PLANES * in_part
                    r_ref[2 * t, rows, at : at + PLANES] = jnp.where(here, hi, 0.0).astype(BF16)
                    r_ref[2 * t + 1, rows, at : at + PLANES] = jnp.where(here, lo, 0.0).astype(BF16)


def exchange(parts):
    piece = lax.broadcasted_iota(jnp.int32, parts[0].shape, 1) // 32
    turned = [x if i == 0 else pltpu.roll(x, 32 * i, 1) for i, x in enumerate(parts)]
    out = []
    for q in range(4):
        x = turned[(3 - q) % 4]
        for p in range(3):
            x = jnp.where(piece == p, turned[(p - q) % 4], x)
        out.append(x if q == 0 else pltpu.roll(x, 128 - 32 * q, 1))
    return out


def middle_kernel(
    rates_ref, ky_ref, g_ref, layer_ref, hi_ref, lo_ref, tw_ref, r_ref, o_ref, line, v_hi, v_lo, l_hi, l_lo, back
):
    cos, sin = tw_ref[0:1, :], tw_ref[1:2, :]
    for group in range(4):
        parts = [g_ref[:, 4 * group + i].reshape(PLANES, 128) for i in range(4)]
        for q, x in enumerate(exchange(parts)):
            line[q // 2, q % 2, :, 128 * group : 128 * (group + 1)] = x
    for ky in (0, 1):
        first = [line[c, ky, :, :HALF] for c in (0, 1)]
        second = [line[c, ky, :, HALF:] for c in (0, 1)]
        odd = [first[c] - second[c] for c in (0, 1)]
        turned = (odd[0] * cos + odd[1] * sin, odd[1] * cos - odd[0] * sin)
        for c in (0, 1):
            rows = slice(PLANES * c, PLANES * (c + 1))
            v_hi[2 * ky, rows], v_lo[2 * ky, rows] = split(first[c] + second[c])
            v_hi[2 * ky + 1, rows], v_lo[2 * ky + 1, rows] = split(turned[c])

    depth = lax.broadcasted_iota(jnp.int32, (HALF, PLANES), 1).astype(F32)
    layer = layer_ref[...]
    rate_here = jnp.zeros((1, PLANES), F32)
    for l in range(LAYERS):
        rate_here = jnp.where(layer == l, rates_ref[l], rate_here)

    def signed(k):
        return jnp.where(k >= HALF, k - 2 * HALF, k).astype(F32) / HALF

    @pl.loop(0, 4)
    def _(g):
        t_hi, t_lo = hi_ref[...], lo_ref[...]
        out = dot3(t_hi, t_lo, v_hi[g], v_lo[g])
        spec_re = out[:HALF, :PLANES] + out[HALF:, PLANES:]
        spec_im = out[:HALF, PLANES:] - out[HALF:, :PLANES]
        kx = 2 * lax.broadcasted_iota(jnp.int32, (HALF, PLANES), 0) + g % 2
        freq_y = signed(jnp.full((HALF, PLANES), 2 * ky_ref[0] + g // 2, jnp.int32))
        steep = jnp.sqrt(1.0 + signed(kx) ** 2 + freq_y**2)
        scaled = steep * depth
        for l in range(LAYERS):
            angle = scaled * (rates_ref[l] / (2 * PLANES))
            half = jnp.exp(-angle)
            factors = (jnp.exp(2.0 * angle), half * half, half)
            for t, factor in enumerate(factors):
                for c, x in enumerate((spec_re, spec_im)):
                    at = 2 * PLANES * l + PLANES * c
                    l_hi[t, :, at : at + PLANES], l_lo[t, :, at : at + PLANES] = split(x * factor)
        angle = scaled * (rate_here / (2 * PLANES))
        half = jnp.exp(-angle)
        factors = (half * half, jnp.exp(2.0 * angle), half)
        mixed = jnp.zeros((HALF, 2 * PLANES), F32)
        for t in range(3):
            sums = dot3(l_hi[t], l_lo[t], r_ref[2 * t], r_ref[2 * t + 1])
            mixed = mixed + sums * jnp.concatenate([factors[t], factors[t]], 1)
        m_hi, m_lo = split(jnp.transpose(mixed))
        inv = dot3(m_hi, m_lo, t_hi, t_lo)
        back[g, 0] = inv[:PLANES, :HALF] - inv[PLANES:, HALF:]
        back[g, 1] = inv[:PLANES, HALF:] + inv[PLANES:, :HALF]

    for ky in (0, 1):
        even = [back[2 * ky, c] for c in (0, 1)]
        odd = [back[2 * ky + 1, c] for c in (0, 1)]
        turned = (odd[0] * cos - odd[1] * sin, odd[0] * sin + odd[1] * cos)
        for c in (0, 1):
            line[c, ky, :, :HALF] = even[c] + turned[c]
            line[c, ky, :, HALF:] = even[c] - turned[c]
    for group in range(4):
        parts = [line[q // 2, q % 2, :, 128 * group : 128 * (group + 1)] for q in range(4)]
        for i, x in enumerate(exchange(parts)):
            o_ref[:, 4 * group + i] = x.reshape(PLANES // 8, 8, 128)


def inverse_y_kernel(g_ref, contrast_ref, hi_ref, lo_ref, tw_ref, o_ref):
    cos, sin = tw_ref[0:1, :], tw_ref[1:2, :]
    t_hi, t_lo = hi_ref[...], lo_ref[...]
    planes = contrast_ref.shape[0]
    scale = 1.0 / (4 * HALF * HALF)
    for pair in range(planes // 2):
        both = [jnp.transpose(g_ref[pl.ds(2 * pair + k, HALF, stride=8), :]) for k in (0, 1)]
        m_hi, m_lo = split(jnp.concatenate(both, 0))
        out = dot3(m_hi, m_lo, t_hi, t_lo)
        for k in (0, 1):
            real, imag = out[128 * k : 128 * k + 64], out[128 * k + 64 : 128 * (k + 1)]
            re = real[:, :HALF] - imag[:, HALF:]
            im = real[:, HALF:] + imag[:, :HALF]
            turned = (re[32:] * cos - im[32:] * sin, re[32:] * sin + im[32:] * cos)
            z = 2 * pair + k
            for c, even in enumerate((re[:32], im[:32])):
                o_ref[c, z, :, :HALF] = (even + turned[c]) * (contrast_ref[z, :, :HALF] * scale)
                o_ref[c, z, :, HALF:] = (even - turned[c]) * (contrast_ref[z, :, HALF:] * scale)


def vmem(count):
    return [pl.BlockSpec(memory_space=pltpu.VMEM)] * count


def call(kernel, out_shape, operands, flops, scalars=0, scratch=(), limit=32):
    return pl.pallas_call(
        kernel,
        out_shape=out_shape,
        in_specs=[pl.BlockSpec(memory_space=pltpu.SMEM)] * scalars + vmem(len(operands) - scalars),
        out_specs=pl.BlockSpec(memory_space=pltpu.VMEM),
        scratch_shapes=list(scratch),
        compiler_params=pltpu.CompilerParams(vmem_limit_bytes=limit * MIB),
        cost_estimate=pl.CostEstimate(flops=flops, bytes_accessed=4 * MIB, transcendentals=0),
    )(*operands)


def body(wave_field, contrast, layer_of_plane, toeplitz_table, hankel_table, layer_rates):
    t_hi, t_lo, turn = dft_tables()
    t_hi, t_lo, turn = jnp.asarray(t_hi), jnp.asarray(t_lo), jnp.asarray(turn)
    dft = (t_hi, t_lo, turn)
    layer_row = layer_of_plane.reshape(1, PLANES)
    toeplitz = jnp.pad(toeplitz_table[:, :, ::-1], ((0, 0), (0, 0), (0, 1)))
    hankel = jnp.pad(hankel_table, ((0, 0), (0, 0), (0, 1)))
    ky_pair = (lax.axis_index("lay") * lax.axis_size("lat") + lax.axis_index("lat")).reshape(1)

    tiles = jax.ShapeDtypeStruct((2 * HALF * 4, 128), F32)
    sent = call(forward_y_kernel, tiles, (wave_field, *dft), 6 * 2**27)
    mixers = call(
        tables_kernel,
        jax.ShapeDtypeStruct((6, 2 * PLANES, LAYERS * 2 * PLANES), BF16),
        (layer_row, toeplitz, hankel),
        2**28,
    )
    lines = lax.all_to_all(sent.reshape(HALF, 8, 128), AXES, 0, 0, tiled=True)
    lines = call(
        middle_kernel,
        jax.ShapeDtypeStruct((16, 16, 8, 128), F32),
        (layer_rates, ky_pair, lines.reshape(16, 16, 8, 128), layer_row, *dft, mixers),
        2**32,
        scalars=2,
        scratch=(
            pltpu.VMEM((2, 2, PLANES, 2 * HALF), F32),
            pltpu.VMEM((4, 2 * PLANES, HALF), BF16),
            pltpu.VMEM((4, 2 * PLANES, HALF), BF16),
            pltpu.VMEM((3, HALF, LAYERS * 2 * PLANES), BF16),
            pltpu.VMEM((3, HALF, LAYERS * 2 * PLANES), BF16),
            pltpu.VMEM((4, 2, PLANES, HALF), F32),
        ),
        limit=40,
    )
    lines = lax.all_to_all(lines.reshape(HALF, 8, 128), AXES, 0, 0, tiled=True)
    return call(
        inverse_y_kernel,
        jax.ShapeDtypeStruct(wave_field.shape, F32),
        (lines.reshape(2 * HALF * 4, 128), contrast, *dft),
        6 * 2**27,
    )


def solution(mesh):
    return jax.shard_map(
        body,
        mesh=mesh,
        in_specs=(P(None, "lay", "lat", None), P("lay", "lat", None), P(), P(), P(), P()),
        out_specs=P(None, "lay", "lat", None),
        check_vma=False,
    )
```

```python
import functools
import math

import jax
import jax.numpy as jnp
import numpy as np
import ml_dtypes
from jax import lax
from jax.experimental import pallas as pl
from jax.experimental.pallas import tpu as pltpu
from jax.sharding import PartitionSpec as P

AXES = ("lay", "lat")
F32 = jnp.float32
BF16 = jnp.bfloat16
HALF = 256
PLANES = 128
LAYERS = 8
WINDOW = 40
MIB = 1 << 20


def split_np(x):
    x = x.astype(np.float32)
    hi = x.astype(ml_dtypes.bfloat16)
    lo = (x - hi.astype(np.float32)).astype(ml_dtypes.bfloat16)
    return hi, lo


def dft_tables():
    index = np.arange(HALF)
    angle = 2.0 * math.pi / HALF * ((index[:, None] * index[None, :]) % HALF)
    hi, lo = split_np(np.concatenate([np.cos(angle), np.sin(angle)], 0))
    turn = 2.0 * math.pi / (2 * HALF) * index
    return hi, lo, np.stack([np.cos(turn), np.sin(turn)]).astype(np.float32)


def split(x):
    hi = x.astype(BF16)
    return hi, (x - hi.astype(F32)).astype(BF16)


def dot_nt(a, b):
    return lax.dot_general(a, b, (((1,), (1,)), ((), ())), preferred_element_type=F32)


def window_of(p):
    return pl.multiple_of((p >> 3) << 3, 8)


def dot_nn(a, b):
    return jnp.dot(a, b, preferred_element_type=F32)


def dot3(a_hi, a_lo, b_hi, b_lo):
    return dot_nt(a_hi, b_hi) + dot_nt(a_hi, b_lo) + dot_nt(a_lo, b_hi)


def forward_y_kernel(w_ref, hi_ref, lo_ref, tw_ref, o_ref):
    cos, sin = tw_ref[0:1, :], tw_ref[1:2, :]
    t_hi, t_lo = hi_ref[...], lo_ref[...]
    lane = lax.broadcasted_iota(jnp.int32, (HALF, 128), 1)
    planes = w_ref.shape[1]
    for pair in range(planes // 2):
        rows = []
        for z in (2 * pair, 2 * pair + 1):
            first = [w_ref[c, z, :, :HALF] for c in (0, 1)]
            second = [w_ref[c, z, :, HALF:] for c in (0, 1)]
            even = [first[c] + second[c] for c in (0, 1)]
            odd = [first[c] - second[c] for c in (0, 1)]
            odd_re = odd[0] * cos + odd[1] * sin
            odd_im = odd[1] * cos - odd[0] * sin
            rows += [even[0], odd_re, even[1], odd_im]
        v_hi, v_lo = split(jnp.concatenate(rows, 0))
        out = dot3(t_hi, t_lo, v_hi, v_lo)
        for k in (0, 1):
            with_cos = out[:HALF, 128 * k : 128 * (k + 1)]
            with_sin = pltpu.roll(out[HALF:, 128 * k : 128 * (k + 1)], 64, 1)
            o_ref[pl.ds(2 * pair + k, HALF, stride=8), :] = with_cos + jnp.where(lane < 64, with_sin, -with_sin)


def tables_kernel(start_ref, toe_ref, han_ref, w_ref, own_ref, plane_rows):
    row = lax.broadcasted_iota(jnp.int32, (PLANES, 2 * PLANES), 0)

    def spread(ref, c, amount):
        x = jnp.zeros((PLANES, 2 * PLANES), F32)
        for l in range(LAYERS):
            x = jnp.where(row >= start_ref[l], ref[c, l : l + 1, :], x)
        for bit in range(7):
            moved = pltpu.roll(x, 2 * PLANES - (1 << bit), 1)
            x = jnp.where(((amount >> bit) & 1) == 1, moved, x)
        return x[:, :PLANES]

    def blocks(re, im):
        return jnp.concatenate([jnp.concatenate([re, -im], 1), jnp.concatenate([im, re], 1)], 0)

    plane_rows[:, PLANES:] = jnp.zeros((4, WINDOW, PLANES), F32)
    for c in (0, 1):
        plane_rows[c, :PLANES] = spread(toe_ref, c, PLANES - 1 - row)
        plane_rows[2 + c, :PLANES] = spread(han_ref, c, row)
    z = lax.broadcasted_iota(jnp.int32, (PLANES, PLANES), 0)
    s = lax.broadcasted_iota(jnp.int32, (PLANES, PLANES), 1)
    first = jnp.zeros((PLANES, PLANES), jnp.int32)
    for l in range(LAYERS):
        first = jnp.where(z >= start_ref[l], start_ref[l], first)
    inside = (s >= first) & (s <= z)
    hi, lo = split(blocks(*(jnp.where(inside, plane_rows[c, :PLANES], 0.0) for c in (0, 1))))
    own_ref[: 2 * PLANES], own_ref[2 * PLANES :] = hi, lo
    j = lax.broadcasted_iota(jnp.int32, (WINDOW, PLANES), 0)
    s = lax.broadcasted_iota(jnp.int32, (WINDOW, PLANES), 1)
    for l in range(LAYERS):
        p = start_ref[l]
        q = window_of(p)
        re, im, hre, him = (plane_rows[i, pl.ds(q, WINDOW), :] for i in range(4))
        later = jnp.maximum(q + j, p - 1)
        before = blocks(jnp.where(s < p, re, 0.0), jnp.where(s < p, im, 0.0))
        after = blocks(jnp.where(s > later, re, 0.0), jnp.where(s > later, im, 0.0))
        hi, lo = split(jnp.concatenate([before, after], 0))
        w_ref[l, : 4 * WINDOW], w_ref[l, 4 * WINDOW : 8 * WINDOW] = hi, lo
        w_ref[l, 8 * WINDOW : 10 * WINDOW], w_ref[l, 10 * WINDOW :] = split(blocks(hre, him))


def exchange(parts):
    piece = lax.broadcasted_iota(jnp.int32, parts[0].shape, 1) // 32
    turned = [x if i == 0 else pltpu.roll(x, 32 * i, 1) for i, x in enumerate(parts)]
    out = []
    for q in range(4):
        x = turned[(3 - q) % 4]
        for p in range(3):
            x = jnp.where(piece == p, turned[(p - q) % 4], x)
        out.append(x if q == 0 else pltpu.roll(x, 128 - 32 * q, 1))
    return out


def middle_kernel(
    rates_ref, start_ref, ky_ref, g_ref, hi_ref, lo_ref, tw_ref, w_ref, own_ref, o_ref, line, v_hi, v_lo, own, mixed, back
):
    cos, sin = tw_ref[0:1, :], tw_ref[1:2, :]
    for group in range(4):
        parts = [g_ref[:, 4 * group + i].reshape(PLANES, 128) for i in range(4)]
        for q, x in enumerate(exchange(parts)):
            line[q // 2, q % 2, :, 128 * group : 128 * (group + 1)] = x
    for ky in (0, 1):
        first = [line[c, ky, :, :HALF] for c in (0, 1)]
        second = [line[c, ky, :, HALF:] for c in (0, 1)]
        odd = [first[c] - second[c] for c in (0, 1)]
        turned = (odd[0] * cos + odd[1] * sin, odd[1] * cos - odd[0] * sin)
        for c in (0, 1):
            rows = slice(PLANES * c, PLANES * (c + 1))
            v_hi[2 * ky, rows], v_lo[2 * ky, rows] = split(first[c] + second[c])
            v_hi[2 * ky + 1, rows], v_lo[2 * ky + 1, rows] = split(turned[c])

    own[:, PLANES:] = jnp.zeros((2, WINDOW, HALF), F32)
    plane = lax.broadcasted_iota(jnp.int32, (PLANES, HALF), 0).astype(F32)
    own_depth = jnp.zeros((PLANES, HALF), F32)
    for l in range(LAYERS):
        p = start_ref[l].astype(F32)
        own_depth = jnp.where(plane >= p, (plane - p) * (rates_ref[l] / PLANES), own_depth)
    window = lax.broadcasted_iota(jnp.int32, (WINDOW, HALF), 0).astype(F32)

    def signed(k):
        return jnp.where(k >= HALF, k - 2 * HALF, k).astype(F32) / HALF

    @pl.loop(0, 4)
    def _(g):
        t_hi, t_lo = hi_ref[...], lo_ref[...]
        out = dot3(v_hi[g], v_lo[g], t_hi, t_lo)
        spec_re = out[:PLANES, :HALF] + out[PLANES:, HALF:]
        spec_im = out[PLANES:, :HALF] - out[:PLANES, HALF:]
        kx = 2 * lax.broadcasted_iota(jnp.int32, (1, HALF), 1) + g % 2
        freq_y = signed(jnp.full((1, HALF), 2 * ky_ref[0] + g // 2, jnp.int32))
        steep = jnp.sqrt(1.0 + signed(kx) ** 2 + freq_y**2)

        def weighted(factor):
            return split(jnp.concatenate([spec_re * factor, spec_im * factor], 0))

        x_hi, x_lo = weighted(jnp.exp(own_depth * steep))
        sums = dot_nn(own_ref[...], x_hi)
        sums = sums[: 2 * PLANES] + sums[2 * PLANES :] + dot_nn(own_ref[: 2 * PLANES], x_lo)
        own[0, :PLANES], own[1, :PLANES] = sums[:PLANES], sums[PLANES:]
        for l in range(LAYERS):
            p = start_ref[l]
            depth = p.astype(F32)
            rate = rates_ref[l] / PLANES
            x_hi, x_lo = weighted(jnp.exp((jnp.abs(plane - depth) * -rate) * steep))
            direct = dot_nn(w_ref[l, : 8 * WINDOW], x_hi)
            direct = direct[: 4 * WINDOW] + direct[4 * WINDOW :] + dot_nn(w_ref[l, : 4 * WINDOW], x_lo)
            x_hi, x_lo = weighted(jnp.exp((plane * (-0.5 * rate)) * steep))
            reflected = dot_nn(w_ref[l, 8 * WINDOW :], x_hi)
            reflected = reflected[: 2 * WINDOW] + reflected[2 * WINDOW :] + dot_nn(w_ref[l, 8 * WINDOW : 10 * WINDOW], x_lo)
            q = window_of(p)
            there = window + q.astype(F32)
            angle = (there - depth) * (rate * steep)
            fade, rise = jnp.exp(-angle), jnp.exp(angle)
            far = jnp.exp(there * (-0.5 * rate * steep))
            for c in (0, 1):
                rows = slice(WINDOW * c, WINDOW * (c + 1))
                near = direct[rows] + own[c, pl.ds(q, WINDOW), :]
                after = direct[2 * WINDOW + WINDOW * c : 3 * WINDOW + WINDOW * c]
                sums = near * fade + after * rise + reflected[rows] * far
                kept = mixed[c, pl.ds(q, 8), :]
                mixed[c, pl.ds(q, 8), :] = jnp.where(there[:8] >= depth, sums[:8], kept)
                mixed[c, pl.ds(pl.multiple_of(q + 8, 8), WINDOW - 8), :] = sums[8:]
        m_hi, m_lo = split(jnp.concatenate([mixed[0, :PLANES], mixed[1, :PLANES]], 0))
        inv = dot3(m_hi, m_lo, t_hi, t_lo)
        back[g, 0] = inv[:PLANES, :HALF] - inv[PLANES:, HALF:]
        back[g, 1] = inv[:PLANES, HALF:] + inv[PLANES:, :HALF]

    for ky in (0, 1):
        even = [back[2 * ky, c] for c in (0, 1)]
        odd = [back[2 * ky + 1, c] for c in (0, 1)]
        turned = (odd[0] * cos - odd[1] * sin, odd[0] * sin + odd[1] * cos)
        for c in (0, 1):
            line[c, ky, :, :HALF] = even[c] + turned[c]
            line[c, ky, :, HALF:] = even[c] - turned[c]
    for group in range(4):
        parts = [line[q // 2, q % 2, :, 128 * group : 128 * (group + 1)] for q in range(4)]
        for i, x in enumerate(exchange(parts)):
            o_ref[:, 4 * group + i] = x.reshape(PLANES // 8, 8, 128)


def inverse_y_kernel(g_ref, contrast_ref, hi_ref, lo_ref, tw_ref, o_ref):
    cos, sin = tw_ref[0:1, :], tw_ref[1:2, :]
    t_hi, t_lo = hi_ref[...], lo_ref[...]
    planes = contrast_ref.shape[0]
    scale = 1.0 / (4 * HALF * HALF)
    for pair in range(planes // 2):
        both = [jnp.transpose(g_ref[pl.ds(2 * pair + k, HALF, stride=8), :]) for k in (0, 1)]
        m_hi, m_lo = split(jnp.concatenate(both, 0))
        out = dot3(m_hi, m_lo, t_hi, t_lo)
        for k in (0, 1):
            real, imag = out[128 * k : 128 * k + 64], out[128 * k + 64 : 128 * (k + 1)]
            re = real[:, :HALF] - imag[:, HALF:]
            im = real[:, HALF:] + imag[:, :HALF]
            turned = (re[32:] * cos - im[32:] * sin, re[32:] * sin + im[32:] * cos)
            z = 2 * pair + k
            for c, even in enumerate((re[:32], im[:32])):
                o_ref[c, z, :, :HALF] = (even + turned[c]) * (contrast_ref[z, :, :HALF] * scale)
                o_ref[c, z, :, HALF:] = (even - turned[c]) * (contrast_ref[z, :, HALF:] * scale)


def vmem(count):
    return [pl.BlockSpec(memory_space=pltpu.VMEM)] * count


def call(kernel, out_shape, operands, flops, scalars=0, scratch=(), limit=16):
    return pl.pallas_call(
        kernel,
        out_shape=out_shape,
        in_specs=[pl.BlockSpec(memory_space=pltpu.SMEM)] * scalars + vmem(len(operands) - scalars),
        out_specs=jax.tree.map(lambda _: pl.BlockSpec(memory_space=pltpu.VMEM), out_shape),
        scratch_shapes=list(scratch),
        compiler_params=pltpu.CompilerParams(vmem_limit_bytes=limit * MIB),
        cost_estimate=pl.CostEstimate(flops=flops, bytes_accessed=4 * MIB, transcendentals=0),
    )(*operands)


def body(wave_field, contrast, layer_of_plane, toeplitz_table, hankel_table, layer_rates):
    t_hi, t_lo, turn = dft_tables()
    t_hi, t_lo, turn = jnp.asarray(t_hi), jnp.asarray(t_lo), jnp.asarray(turn)
    dft = (t_hi, t_lo, turn)
    ids = jnp.arange(LAYERS, dtype=jnp.int32)
    starts = jnp.sum((layer_of_plane[None, :] < ids[:, None]).astype(jnp.int32), axis=1)
    toeplitz = jnp.pad(toeplitz_table[:, :, ::-1], ((0, 0), (0, 0), (0, 1)))
    hankel = jnp.pad(hankel_table, ((0, 0), (0, 0), (0, 1)))
    ky_pair = (lax.axis_index("lay") * lax.axis_size("lat") + lax.axis_index("lat")).reshape(1)

    tiles = jax.ShapeDtypeStruct((2 * HALF * 4, 128), F32)
    sent = call(forward_y_kernel, tiles, (wave_field, *dft), 6 * 2**27)
    window_mix, own_mix = call(
        tables_kernel,
        (
            jax.ShapeDtypeStruct((LAYERS, 12 * WINDOW, 2 * PLANES), BF16),
            jax.ShapeDtypeStruct((4 * PLANES, 2 * PLANES), BF16),
        ),
        (starts, toeplitz, hankel),
        2**28,
        scalars=1,
        scratch=(pltpu.VMEM((4, PLANES + WINDOW, PLANES), F32),),
        limit=12,
    )
    lines = lax.all_to_all(sent.reshape(HALF, 8, 128), AXES, 0, 0, tiled=True)
    lines = call(
        middle_kernel,
        jax.ShapeDtypeStruct((16, 16, 8, 128), F32),
        (layer_rates, starts, ky_pair, lines.reshape(16, 16, 8, 128), *dft, window_mix, own_mix),
        2**32,
        scalars=3,
        scratch=(
            pltpu.VMEM((2, 2, PLANES, 2 * HALF), F32),
            pltpu.VMEM((4, 2 * PLANES, HALF), BF16),
            pltpu.VMEM((4, 2 * PLANES, HALF), BF16),
            pltpu.VMEM((2, PLANES + WINDOW, HALF), F32),
            pltpu.VMEM((2, PLANES + WINDOW, HALF), F32),
            pltpu.VMEM((4, 2, PLANES, HALF), F32),
        ),
        limit=20,
    )
    lines = lax.all_to_all(lines.reshape(HALF, 8, 128), AXES, 0, 0, tiled=True)
    return call(
        inverse_y_kernel,
        jax.ShapeDtypeStruct(wave_field.shape, F32),
        (lines.reshape(2 * HALF * 4, 128), contrast, *dft),
        6 * 2**27,
    )


def solution(mesh):
    return jax.shard_map(
        body,
        mesh=mesh,
        in_specs=(P(None, "lay", "lat", None), P("lay", "lat", None), P(), P(), P(), P()),
        out_specs=P(None, "lay", "lat", None),
        check_vma=False,
    )
```

```python
import math

import jax
import jax.numpy as jnp
import numpy as np
import ml_dtypes
from jax import lax
from jax.experimental import pallas as pl
from jax.experimental.pallas import tpu as pltpu
from jax.sharding import PartitionSpec as P

AXES = ("lay", "lat")
F32 = jnp.float32
BF16 = jnp.bfloat16
HALF = 256
PLANES = 128
LAYERS = 8
WINDOW = 40
MIB = 1 << 20

FACTOR_ROWS = 2 * PLANES + 3 * WINDOW
ALL_FACTOR_ROWS = FACTOR_ROWS * LAYERS + PLANES


def split_np(x):
    x = x.astype(np.float32)
    hi = x.astype(ml_dtypes.bfloat16)
    lo = (x - hi.astype(np.float32)).astype(ml_dtypes.bfloat16)
    return hi, lo


def dft_tables():
    index = np.arange(HALF)
    angle = 2.0 * math.pi / HALF * ((index[:, None] * index[None, :]) % HALF)
    hi, lo = split_np(np.concatenate([np.cos(angle), np.sin(angle)], 0))
    turn = 2.0 * math.pi / (2 * HALF) * index
    return np.concatenate([hi, lo], 0), np.stack([np.cos(turn), np.sin(turn)]).astype(np.float32)


def split(x):
    hi = x.astype(BF16)
    return hi, (x - hi.astype(F32)).astype(BF16)


def dot_nt(a, b):
    return lax.dot_general(a, b, (((1,), (1,)), ((), ())), preferred_element_type=F32)


def window_of(p):
    return pl.multiple_of((p >> 3) << 3, 8)


def dot_nn(a, b):
    return jnp.dot(a, b, preferred_element_type=F32)


def dot3(a_hi, a_lo, b_hi, b_lo):
    return dot_nt(a_hi, b_hi) + dot_nt(a_hi, b_lo) + dot_nt(a_lo, b_hi)


def forward_y_kernel(w_hbm, table_hbm, tw_hbm, o_ref, w_ref, table_ref, tw_ref, sems):
    pairs = w_ref.shape[1] // 2
    copies = [
        pltpu.make_async_copy(w_hbm.at[:, pl.ds(2 * i, 2)], w_ref.at[:, pl.ds(2 * i, 2)], sems.at[i]) for i in range(pairs)
    ]
    fetch_tw = pltpu.make_async_copy(tw_hbm, tw_ref, sems.at[pairs])
    fetch_table = pltpu.make_async_copy(table_hbm, table_ref, sems.at[pairs + 1])
    for copy in (copies[0], fetch_tw, fetch_table, *copies[1:]):
        copy.start()
    fetch_tw.wait()
    fetch_table.wait()
    cos, sin = tw_ref[0:1, :], tw_ref[1:2, :]
    t_hi, t_lo = table_ref[: 2 * HALF], table_ref[2 * HALF :]
    lane = lax.broadcasted_iota(jnp.int32, (HALF, 128), 1)
    for pair in range(pairs):
        copies[pair].wait()
        rows = []
        for z in (2 * pair, 2 * pair + 1):
            first = [w_ref[c, z, :, :HALF] for c in (0, 1)]
            second = [w_ref[c, z, :, HALF:] for c in (0, 1)]
            even = [first[c] + second[c] for c in (0, 1)]
            odd = [first[c] - second[c] for c in (0, 1)]
            odd_re = odd[0] * cos + odd[1] * sin
            odd_im = odd[1] * cos - odd[0] * sin
            rows += [even[0], odd_re, even[1], odd_im]
        v_hi, v_lo = split(jnp.concatenate(rows, 0))
        out = dot3(t_hi, t_lo, v_hi, v_lo)
        for k in (0, 1):
            with_cos = out[:HALF, 128 * k : 128 * (k + 1)]
            with_sin = pltpu.roll(out[HALF:, 128 * k : 128 * (k + 1)], 64, 1)
            o_ref[pl.ds(2 * pair + k, HALF, stride=8), :] = with_cos + jnp.where(lane < 64, with_sin, -with_sin)


def tables_kernel(start_ref, toe_ref, han_ref, w_ref, own_ref, plane_rows):
    row = lax.broadcasted_iota(jnp.int32, (PLANES, 2 * PLANES), 0)

    def spread(ref, c, amount):
        x = jnp.zeros((PLANES, 2 * PLANES), F32)
        for l in range(LAYERS):
            x = jnp.where(row >= start_ref[l], ref[c, l : l + 1, :], x)
        for bit in range(7):
            moved = pltpu.roll(x, 2 * PLANES - (1 << bit), 1)
            x = jnp.where(((amount >> bit) & 1) == 1, moved, x)
        return x[:, :PLANES]

    def blocks(re, im):
        return jnp.concatenate([jnp.concatenate([re, -im], 1), jnp.concatenate([im, re], 1)], 0)

    plane_rows[:, PLANES:] = jnp.zeros((4, WINDOW, PLANES), F32)
    for c in (0, 1):
        plane_rows[c, :PLANES] = spread(toe_ref, c, PLANES - 1 - row)
        plane_rows[2 + c, :PLANES] = spread(han_ref, c, row)
    z = lax.broadcasted_iota(jnp.int32, (PLANES, PLANES), 0)
    s = lax.broadcasted_iota(jnp.int32, (PLANES, PLANES), 1)
    first = jnp.zeros((PLANES, PLANES), jnp.int32)
    for l in range(LAYERS):
        first = jnp.where(z >= start_ref[l], start_ref[l], first)
    inside = (s >= first) & (s <= z)
    hi, lo = split(blocks(*(jnp.where(inside, plane_rows[c, :PLANES], 0.0) for c in (0, 1))))
    own_ref[: 2 * PLANES], own_ref[2 * PLANES :] = hi, lo
    j = lax.broadcasted_iota(jnp.int32, (WINDOW, PLANES), 0)
    s = lax.broadcasted_iota(jnp.int32, (WINDOW, PLANES), 1)
    for l in range(LAYERS):
        p = start_ref[l]
        q = window_of(p)
        re, im, hre, him = (plane_rows[i, pl.ds(q, WINDOW), :] for i in range(4))
        later = jnp.maximum(q + j, p - 1)
        before = blocks(jnp.where(s < p, re, 0.0), jnp.where(s < p, im, 0.0))
        after = blocks(jnp.where(s > later, re, 0.0), jnp.where(s > later, im, 0.0))
        hi, lo = split(jnp.concatenate([before, after], 0))
        w_ref[l, : 4 * WINDOW], w_ref[l, 4 * WINDOW : 8 * WINDOW] = hi, lo
        w_ref[l, 8 * WINDOW : 10 * WINDOW], w_ref[l, 10 * WINDOW :] = split(blocks(hre, him))


def factors_kernel(rates_ref, start_ref, ky_ref, f_ref):
    g = pl.program_id(0)

    def signed(k):
        return jnp.where(k >= HALF, k - 2 * HALF, k).astype(F32) / HALF

    kx = 2 * lax.broadcasted_iota(jnp.int32, (1, HALF), 1) + g % 2
    freq_y = signed(jnp.full((1, HALF), 2 * ky_ref[0] + g // 2, jnp.int32))
    steep = jnp.sqrt(1.0 + signed(kx) ** 2 + freq_y**2)
    plane = lax.broadcasted_iota(jnp.int32, (PLANES, HALF), 0).astype(F32)
    window = lax.broadcasted_iota(jnp.int32, (WINDOW, HALF), 0).astype(F32)
    own_depth = jnp.zeros((PLANES, HALF), F32)
    for l in range(LAYERS):
        depth = start_ref[l].astype(F32)
        rate = rates_ref[l] / PLANES
        own_depth = jnp.where(plane >= depth, (plane - depth) * rate, own_depth)
        fall = rate * steep
        at = FACTOR_ROWS * l
        f_ref[0, at : at + PLANES] = jnp.exp(-jnp.abs(plane - depth) * fall)
        f_ref[0, at + PLANES : at + 2 * PLANES] = jnp.exp(plane * (-0.5 * fall))
        there = window + window_of(start_ref[l]).astype(F32)
        at += 2 * PLANES
        f_ref[0, at : at + WINDOW] = jnp.exp((depth - there) * fall)
        f_ref[0, at + WINDOW : at + 2 * WINDOW] = jnp.exp((there - depth) * fall)
        f_ref[0, at + 2 * WINDOW : at + 3 * WINDOW] = jnp.exp(there * (-0.5 * fall))
    f_ref[0, FACTOR_ROWS * LAYERS :] = jnp.exp(own_depth * steep)


def exchange(parts):
    piece = lax.broadcasted_iota(jnp.int32, parts[0].shape, 1) // 32
    turned = [x if i == 0 else pltpu.roll(x, 32 * i, 1) for i, x in enumerate(parts)]
    out = []
    for q in range(4):
        x = turned[(3 - q) % 4]
        for p in range(3):
            x = jnp.where(piece == p, turned[(p - q) % 4], x)
        out.append(x if q == 0 else pltpu.roll(x, 128 - 32 * q, 1))
    return out


def middle_kernel(
    start_ref,
    g_ref,
    table_ref,
    tw_ref,
    w_hbm,
    own_hbm,
    f_hbm,
    o_ref,
    line,
    spec,
    own,
    mixed,
    back,
    w_ref,
    own_ref,
    f_ref,
    sems,
):
    fetch_factors = [pltpu.make_async_copy(f_hbm.at[g], f_ref.at[g], sems.at[g]) for g in range(4)]
    fetch_mix = pltpu.make_async_copy(w_hbm, w_ref, sems.at[4])
    fetch_own = pltpu.make_async_copy(own_hbm, own_ref, sems.at[5])
    for copy in (fetch_own, fetch_factors[0], fetch_mix, *fetch_factors[1:]):
        copy.start()
    cos, sin = tw_ref[0:1, :], tw_ref[1:2, :]
    t_hi, t_lo = table_ref[: 2 * HALF], table_ref[2 * HALF :]
    for group in range(4):
        parts = [g_ref[:, 4 * group + i].reshape(PLANES, 128) for i in range(4)]
        for q, x in enumerate(exchange(parts)):
            line[q // 2, q % 2, :, 128 * group : 128 * (group + 1)] = x
    for ky in (0, 1):
        first = [line[c, ky, :, :HALF] for c in (0, 1)]
        second = [line[c, ky, :, HALF:] for c in (0, 1)]
        even = [first[c] + second[c] for c in (0, 1)]
        odd = [first[c] - second[c] for c in (0, 1)]
        turned = (odd[0] * cos + odd[1] * sin, odd[1] * cos - odd[0] * sin)
        for parity, x in enumerate((even, turned)):
            x_hi, x_lo = split(jnp.concatenate(x, 0))
            out = dot3(x_hi, x_lo, t_hi, t_lo)
            spec[2 * ky + parity, 0] = out[:PLANES, :HALF] + out[PLANES:, HALF:]
            spec[2 * ky + parity, 1] = out[PLANES:, :HALF] - out[:PLANES, HALF:]

    own[:, PLANES:] = jnp.zeros((2, WINDOW, HALF), F32)
    plane = lax.broadcasted_iota(jnp.int32, (8, HALF), 0)
    fetch_own.wait()
    fetch_mix.wait()

    @pl.loop(0, 4)
    def _(g):
        pltpu.make_async_copy(f_hbm.at[g], f_ref.at[g], sems.at[g]).wait()

        def weighted(at):
            factor = f_ref[g, at : at + PLANES]
            return split(jnp.concatenate([spec[g, 0] * factor, spec[g, 1] * factor], 0))

        x_hi, x_lo = weighted(FACTOR_ROWS * LAYERS)
        sums = dot_nn(own_ref[...], x_hi)
        sums = sums[: 2 * PLANES] + sums[2 * PLANES :] + dot_nn(own_ref[: 2 * PLANES], x_lo)
        own[0, :PLANES], own[1, :PLANES] = sums[:PLANES], sums[PLANES:]
        for l in range(LAYERS):
            at = FACTOR_ROWS * l
            x_hi, x_lo = weighted(at)
            direct = dot_nn(w_ref[l, : 8 * WINDOW], x_hi)
            direct = direct[: 4 * WINDOW] + direct[4 * WINDOW :] + dot_nn(w_ref[l, : 4 * WINDOW], x_lo)
            x_hi, x_lo = weighted(at + PLANES)
            reflected = dot_nn(w_ref[l, 8 * WINDOW :], x_hi)
            reflected = reflected[: 2 * WINDOW] + reflected[2 * WINDOW :] + dot_nn(w_ref[l, 8 * WINDOW : 10 * WINDOW], x_lo)
            p = start_ref[l]
            q = window_of(p)
            at += 2 * PLANES
            fade, rise, far = (f_ref[g, at + WINDOW * i : at + WINDOW * (i + 1)] for i in range(3))
            for c in (0, 1):
                rows = slice(WINDOW * c, WINDOW * (c + 1))
                near = direct[rows] + own[c, pl.ds(q, WINDOW), :]
                after = direct[2 * WINDOW + WINDOW * c : 3 * WINDOW + WINDOW * c]
                sums = near * fade + after * rise + reflected[rows] * far
                kept = mixed[c, pl.ds(q, 8), :]
                mixed[c, pl.ds(q, 8), :] = jnp.where(plane + q >= p, sums[:8], kept)
                mixed[c, pl.ds(pl.multiple_of(q + 8, 8), WINDOW - 8), :] = sums[8:]
        for c in (0, 1):
            back[g, c] = mixed[c, :PLANES]

    for ky in (0, 1):
        halves = []
        for parity in (0, 1):
            m_hi, m_lo = split(jnp.concatenate([back[2 * ky + parity, 0], back[2 * ky + parity, 1]], 0))
            inv = dot3(m_hi, m_lo, t_hi, t_lo)
            halves.append((inv[:PLANES, :HALF] - inv[PLANES:, HALF:], inv[:PLANES, HALF:] + inv[PLANES:, :HALF]))
        even, odd = halves
        turned = (odd[0] * cos - odd[1] * sin, odd[0] * sin + odd[1] * cos)
        for c in (0, 1):
            line[c, ky, :, :HALF] = even[c] + turned[c]
            line[c, ky, :, HALF:] = even[c] - turned[c]
    for group in range(4):
        parts = [line[q // 2, q % 2, :, 128 * group : 128 * (group + 1)] for q in range(4)]
        for i, x in enumerate(exchange(parts)):
            o_ref[:, 4 * group + i] = x.reshape(PLANES // 8, 8, 128)


def inverse_y_kernel(g_ref, contrast_ref, table_ref, tw_ref, o_hbm, o_ref, sems):
    cos, sin = tw_ref[0:1, :], tw_ref[1:2, :]
    t_hi, t_lo = table_ref[: 2 * HALF], table_ref[2 * HALF :]
    copies = []
    planes = contrast_ref.shape[0]
    scale = 1.0 / (4 * HALF * HALF)
    for pair in range(planes // 2):
        both = [jnp.transpose(g_ref[pl.ds(2 * pair + k, HALF, stride=8), :]) for k in (0, 1)]
        m_hi, m_lo = split(jnp.concatenate(both, 0))
        out = dot3(m_hi, m_lo, t_hi, t_lo)
        for k in (0, 1):
            real, imag = out[128 * k : 128 * k + 64], out[128 * k + 64 : 128 * (k + 1)]
            re = real[:, :HALF] - imag[:, HALF:]
            im = real[:, HALF:] + imag[:, :HALF]
            turned = (re[32:] * cos - im[32:] * sin, re[32:] * sin + im[32:] * cos)
            z = 2 * pair + k
            for c, even in enumerate((re[:32], im[:32])):
                o_ref[c, z, :, :HALF] = (even + turned[c]) * (contrast_ref[z, :, :HALF] * scale)
                o_ref[c, z, :, HALF:] = (even - turned[c]) * (contrast_ref[z, :, HALF:] * scale)
        here = pl.ds(2 * pair, 2)
        copies.append(pltpu.make_async_copy(o_ref.at[:, here], o_hbm.at[:, here], sems.at[pair]))
        copies[-1].start()
    for copy in copies:
        copy.wait()


VMEM = pl.BlockSpec(memory_space=pltpu.VMEM)
SMEM = pl.BlockSpec(memory_space=pltpu.SMEM)
HBM = pl.BlockSpec(memory_space=pltpu.HBM)


def call(kernel, out_shape, operands, in_specs, out_specs, flops, scratch=(), limit=16, grid=()):
    operands = [pltpu.with_memory_space_constraint(x, pltpu.HBM) if spec is HBM else x for x, spec in zip(operands, in_specs)]
    return pl.pallas_call(
        kernel,
        grid=grid,
        out_shape=out_shape,
        in_specs=in_specs,
        out_specs=out_specs,
        scratch_shapes=list(scratch),
        compiler_params=pltpu.CompilerParams(vmem_limit_bytes=limit * MIB),
        cost_estimate=pl.CostEstimate(flops=flops, bytes_accessed=4 * MIB, transcendentals=0),
    )(*operands)


def body(wave_field, contrast, layer_of_plane, toeplitz_table, hankel_table, layer_rates):
    table, turn = (jnp.asarray(x) for x in dft_tables())
    ids = jnp.arange(LAYERS, dtype=jnp.int32)
    starts = jnp.sum((layer_of_plane[None, :] < ids[:, None]).astype(jnp.int32), axis=1)
    toeplitz = jnp.pad(toeplitz_table[:, :, ::-1], ((0, 0), (0, 0), (0, 1)))
    hankel = jnp.pad(hankel_table, ((0, 0), (0, 0), (0, 1)))
    ky_pair = (lax.axis_index("lay") * lax.axis_size("lat") + lax.axis_index("lat")).reshape(1)
    planes = contrast.shape[0]
    shape = jax.ShapeDtypeStruct
    dma = pltpu.SemaphoreType.DMA

    sent = call(
        forward_y_kernel,
        shape((2 * HALF * 4, 128), F32),
        (wave_field, table, turn),
        [HBM] * 3,
        VMEM,
        6 * 2**27,
        scratch=(
            pltpu.VMEM(wave_field.shape, F32),
            pltpu.VMEM(table.shape, BF16),
            pltpu.VMEM(turn.shape, F32),
            dma((planes // 2 + 2,)),
        ),
    )
    window_mix, own_mix = call(
        tables_kernel,
        (shape((LAYERS, 12 * WINDOW, 2 * PLANES), BF16), shape((4 * PLANES, 2 * PLANES), BF16)),
        (starts, toeplitz, hankel),
        [SMEM, VMEM, VMEM],
        (VMEM, VMEM),
        2**30,
        scratch=(pltpu.VMEM((4, PLANES + WINDOW, PLANES), F32),),
    )
    factors = call(
        factors_kernel,
        shape((4, ALL_FACTOR_ROWS, HALF), F32),
        (layer_rates, starts, ky_pair),
        [SMEM] * 3,
        pl.BlockSpec((1, ALL_FACTOR_ROWS, HALF), lambda g: (g, 0, 0)),
        2**32,
        grid=(4,),
    )
    lines = lax.all_to_all(sent.reshape(HALF, 8, 128), AXES, 0, 0, tiled=True)
    lines = call(
        middle_kernel,
        shape((16, 16, 8, 128), F32),
        (starts, lines.reshape(16, 16, 8, 128), table, turn, window_mix, own_mix, factors),
        [SMEM, VMEM, VMEM, VMEM, HBM, HBM, HBM],
        VMEM,
        2**32,
        scratch=(
            pltpu.VMEM((2, 2, PLANES, 2 * HALF), F32),
            pltpu.VMEM((4, 2, PLANES, HALF), F32),
            pltpu.VMEM((2, PLANES + WINDOW, HALF), F32),
            pltpu.VMEM((2, PLANES + WINDOW, HALF), F32),
            pltpu.VMEM((4, 2, PLANES, HALF), F32),
            pltpu.VMEM(window_mix.shape, BF16),
            pltpu.VMEM(own_mix.shape, BF16),
            pltpu.VMEM(factors.shape, F32),
            dma((6,)),
        ),
        limit=32,
    )
    lines = lax.all_to_all(lines.reshape(HALF, 8, 128), AXES, 0, 0, tiled=True)
    return call(
        inverse_y_kernel,
        shape(wave_field.shape, F32),
        (lines.reshape(2 * HALF * 4, 128), contrast, table, turn),
        [VMEM] * 4,
        HBM,
        6 * 2**27,
        scratch=(pltpu.VMEM(wave_field.shape, F32), dma((planes // 2,))),
    )


def solution(mesh):
    return jax.shard_map(
        body,
        mesh=mesh,
        in_specs=(P(None, "lay", "lat", None), P("lay", "lat", None), P(), P(), P(), P()),
        out_specs=P(None, "lay", "lat", None),
        check_vma=False,
    )
```

```python
import math

import jax
import jax.numpy as jnp
import numpy as np
import ml_dtypes
from jax import lax
from jax.experimental import pallas as pl
from jax.experimental.pallas import tpu as pltpu
from jax.sharding import PartitionSpec as P

AXES = ("lay", "lat")
F32 = jnp.float32
BF16 = jnp.bfloat16
HALF = 256
PLANES = 128
LAYERS = 8
WINDOW = 40
MIB = 1 << 20

FACTOR_ROWS = 2 * PLANES + 3 * WINDOW
ALL_FACTOR_ROWS = FACTOR_ROWS * LAYERS + PLANES
MIX_ROWS = 12 * WINDOW
OWN_AT = MIX_ROWS * LAYERS
SENDS = 2


def split_np(x):
    x = x.astype(np.float32)
    hi = x.astype(ml_dtypes.bfloat16)
    lo = (x - hi.astype(np.float32)).astype(ml_dtypes.bfloat16)
    return hi, lo


def dft_tables():
    index = np.arange(HALF)
    angle = 2.0 * math.pi / HALF * ((index[:, None] * index[None, :]) % HALF)
    hi, lo = split_np(np.concatenate([np.cos(angle), np.sin(angle)], 0))
    turn = 2.0 * math.pi / (2 * HALF) * index
    return np.concatenate([hi, lo], 0), np.stack([np.cos(turn), np.sin(turn)]).astype(np.float32)


def split(x):
    hi = x.astype(BF16)
    return hi, (x - hi.astype(F32)).astype(BF16)


def dot_nt(a, b):
    return lax.dot_general(a, b, (((1,), (1,)), ((), ())), preferred_element_type=F32)


def window_of(p):
    return pl.multiple_of((p >> 3) << 3, 8)


def dot_nn(a, b):
    return jnp.dot(a, b, preferred_element_type=F32)


def dot3(a_hi, a_lo, b_hi, b_lo):
    return dot_nt(a_hi, b_hi) + dot_nt(a_hi, b_lo) + dot_nt(a_lo, b_hi)


def forward_y_kernel(w_hbm, table_hbm, tw_hbm, o_hbm, w_ref, table_ref, tw_ref, v_hi, v_lo, o_ref, sems):
    pairs = w_ref.shape[1] // 2
    copies = [
        pltpu.make_async_copy(w_hbm.at[:, pl.ds(2 * i, 2)], w_ref.at[:, pl.ds(2 * i, 2)], sems.at[i]) for i in range(pairs)
    ]
    fetch_tw = pltpu.make_async_copy(tw_hbm, tw_ref, sems.at[pairs])
    fetch_table = pltpu.make_async_copy(table_hbm, table_ref, sems.at[pairs + 1])
    for copy in (fetch_tw, copies[0], fetch_table, *copies[1:]):
        copy.start()
    fetch_tw.wait()
    cos, sin = tw_ref[0:1, :], tw_ref[1:2, :]
    for pair in range(pairs):
        copies[pair].wait()
        rows = []
        for z in (2 * pair, 2 * pair + 1):
            first = [w_ref[c, z, :, :HALF] for c in (0, 1)]
            second = [w_ref[c, z, :, HALF:] for c in (0, 1)]
            even = [first[c] + second[c] for c in (0, 1)]
            odd = [first[c] - second[c] for c in (0, 1)]
            odd_re = odd[0] * cos + odd[1] * sin
            odd_im = odd[1] * cos - odd[0] * sin
            rows += [even[0], odd_re, even[1], odd_im]
        v_hi[pair], v_lo[pair] = split(jnp.concatenate(rows, 0))
    fetch_table.wait()
    count = HALF // SENDS
    lane = lax.broadcasted_iota(jnp.int32, (count, 128), 1)
    sends = []
    for part in range(SENDS):
        cos_rows, sin_rows = slice(count * part, count * (part + 1)), slice(HALF + count * part, HALF + count * (part + 1))
        t_hi = jnp.concatenate([table_ref[cos_rows], table_ref[sin_rows]], 0)
        low = 2 * HALF
        t_lo = jnp.concatenate([table_ref[low + rows.start : low + rows.stop] for rows in (cos_rows, sin_rows)], 0)
        for pair in range(pairs):
            out = dot3(t_hi, t_lo, v_hi[pair], v_lo[pair])
            for k in (0, 1):
                with_cos = out[:count, 128 * k : 128 * (k + 1)]
                with_sin = pltpu.roll(out[count:, 128 * k : 128 * (k + 1)], 64, 1)
                o_ref[pl.ds(8 * count * part + 2 * pair + k, count, stride=8), :] = with_cos + jnp.where(
                    lane < 64, with_sin, -with_sin
                )
        here = pl.ds(8 * count * part, 8 * count)
        sends.append(pltpu.make_async_copy(o_ref.at[here], o_hbm.at[here], sems.at[pairs + 2 + part]))
        sends[-1].start()
    for send in sends:
        send.wait()


def tables_kernel(start_ref, toe_ref, han_ref, mix_ref, same_start_ref, plane_rows):
    row = lax.broadcasted_iota(jnp.int32, (PLANES, 2 * PLANES), 0)

    def spread(ref, c, amount):
        x = jnp.zeros((PLANES, 2 * PLANES), F32)
        for l in range(LAYERS):
            x = jnp.where(row >= start_ref[l], ref[c, l : l + 1, :], x)
        for bit in range(7):
            moved = pltpu.roll(x, 2 * PLANES - (1 << bit), 1)
            x = jnp.where(((amount >> bit) & 1) == 1, moved, x)
        return x[:, :PLANES]

    def blocks(re, im):
        return jnp.concatenate([jnp.concatenate([re, -im], 1), jnp.concatenate([im, re], 1)], 0)

    plane_rows[:, PLANES:] = jnp.zeros((4, WINDOW, PLANES), F32)
    for c in (0, 1):
        plane_rows[c, :PLANES] = spread(toe_ref, c, PLANES - 1 - row)
        plane_rows[2 + c, :PLANES] = spread(han_ref, c, row)
    z = lax.broadcasted_iota(jnp.int32, (PLANES, PLANES), 0)
    s = lax.broadcasted_iota(jnp.int32, (PLANES, PLANES), 1)
    first = jnp.zeros((PLANES, PLANES), jnp.int32)
    for l in range(LAYERS):
        first = jnp.where(z >= start_ref[l], start_ref[l], first)
    inside = (s >= first) & (s <= z)
    hi, lo = split(blocks(*(jnp.where(inside, plane_rows[c, :PLANES], 0.0) for c in (0, 1))))
    mix_ref[OWN_AT : OWN_AT + 2 * PLANES], mix_ref[OWN_AT + 2 * PLANES :] = hi, lo
    j = lax.broadcasted_iota(jnp.int32, (WINDOW, PLANES), 0)
    s = lax.broadcasted_iota(jnp.int32, (WINDOW, PLANES), 1)
    for l in range(LAYERS):
        p = start_ref[l]
        q = window_of(p)
        re, im, hre, him = (plane_rows[i, pl.ds(q, WINDOW), :] for i in range(4))
        later = jnp.maximum(q + j, p - 1)
        before = blocks(jnp.where(s < p, re, 0.0), jnp.where(s < p, im, 0.0))
        after = blocks(jnp.where(s > later, re, 0.0), jnp.where(s > later, im, 0.0))
        hi, lo = split(jnp.concatenate([before, after], 0))
        at = MIX_ROWS * l
        mix_ref[at : at + 4 * WINDOW], mix_ref[at + 4 * WINDOW : at + 8 * WINDOW] = hi, lo
        mix_ref[at + 8 * WINDOW : at + 10 * WINDOW], mix_ref[at + 10 * WINDOW : at + 12 * WINDOW] = split(blocks(hre, him))
        same_start_ref[l] = p


def factors_kernel(rates_ref, start_ref, ky_ref, f_ref):
    g = pl.program_id(0)

    def signed(k):
        return jnp.where(k >= HALF, k - 2 * HALF, k).astype(F32) / HALF

    kx = 2 * lax.broadcasted_iota(jnp.int32, (1, HALF), 1) + g % 2
    freq_y = signed(jnp.full((1, HALF), 2 * ky_ref[0] + g // 2, jnp.int32))
    steep = jnp.sqrt(1.0 + signed(kx) ** 2 + freq_y**2)
    plane = lax.broadcasted_iota(jnp.int32, (PLANES, HALF), 0).astype(F32)
    window = lax.broadcasted_iota(jnp.int32, (WINDOW, HALF), 0).astype(F32)
    own_depth = jnp.zeros((PLANES, HALF), F32)
    for l in range(LAYERS):
        depth = start_ref[l].astype(F32)
        rate = rates_ref[l] / PLANES
        own_depth = jnp.where(plane >= depth, (plane - depth) * rate, own_depth)
        fall = rate * steep
        at = FACTOR_ROWS * l
        f_ref[0, at : at + PLANES] = jnp.exp(-jnp.abs(plane - depth) * fall)
        f_ref[0, at + PLANES : at + 2 * PLANES] = jnp.exp(plane * (-0.5 * fall))
        there = window + window_of(start_ref[l]).astype(F32)
        at += 2 * PLANES
        f_ref[0, at : at + WINDOW] = jnp.exp((depth - there) * fall)
        f_ref[0, at + WINDOW : at + 2 * WINDOW] = jnp.exp((there - depth) * fall)
        f_ref[0, at + 2 * WINDOW : at + 3 * WINDOW] = jnp.exp(there * (-0.5 * fall))
    f_ref[0, FACTOR_ROWS * LAYERS :] = jnp.exp(own_depth * steep)


def exchange(parts):
    piece = lax.broadcasted_iota(jnp.int32, parts[0].shape, 1) // 32
    turned = [x if i == 0 else pltpu.roll(x, 32 * i, 1) for i, x in enumerate(parts)]
    out = []
    for q in range(4):
        x = turned[(3 - q) % 4]
        for p in range(3):
            x = jnp.where(piece == p, turned[(p - q) % 4], x)
        out.append(x if q == 0 else pltpu.roll(x, 128 - 32 * q, 1))
    return out


def middle_kernel(
    start_ref,
    g_ref,
    table_hbm,
    tw_ref,
    mix_ref,
    f_hbm,
    o_ref,
    line,
    spec,
    own,
    mixed,
    f_ref,
    table_ref,
    sems,
):
    fetch_table = pltpu.make_async_copy(table_hbm, table_ref, sems.at[4])
    fetch_table.start()
    for g in range(4):
        pltpu.make_async_copy(f_hbm.at[g], f_ref.at[g], sems.at[g]).start()
    cos, sin = tw_ref[0:1, :], tw_ref[1:2, :]
    for group in range(4):
        parts = [g_ref[:, 4 * group + i].reshape(PLANES, 128) for i in range(4)]
        for q, x in enumerate(exchange(parts)):
            line[q // 2, q % 2, :, 128 * group : 128 * (group + 1)] = x
    fetch_table.wait()
    t_hi, t_lo = table_ref[: 2 * HALF], table_ref[2 * HALF :]
    for ky in (0, 1):
        first = [line[c, ky, :, :HALF] for c in (0, 1)]
        second = [line[c, ky, :, HALF:] for c in (0, 1)]
        even = [first[c] + second[c] for c in (0, 1)]
        odd = [first[c] - second[c] for c in (0, 1)]
        turned = (odd[0] * cos + odd[1] * sin, odd[1] * cos - odd[0] * sin)
        for parity, x in enumerate((even, turned)):
            x_hi, x_lo = split(jnp.concatenate(x, 0))
            out = dot3(x_hi, x_lo, t_hi, t_lo)
            spec[2 * ky + parity, 0] = out[:PLANES, :HALF] + out[PLANES:, HALF:]
            spec[2 * ky + parity, 1] = out[PLANES:, :HALF] - out[:PLANES, HALF:]

    own[:, :, PLANES:] = jnp.zeros((4, 2, WINDOW, HALF), F32)
    plane = lax.broadcasted_iota(jnp.int32, (8, HALF), 0)

    @pl.loop(0, 4)
    def _(g):
        pltpu.make_async_copy(f_hbm.at[g], f_ref.at[g], sems.at[g]).wait()

        def weighted(at):
            factor = f_ref[g, at : at + PLANES]
            return split(jnp.concatenate([spec[g, 0] * factor, spec[g, 1] * factor], 0))

        x_hi, x_lo = weighted(FACTOR_ROWS * LAYERS)
        sums = dot_nn(mix_ref[OWN_AT:], x_hi)
        sums = sums[: 2 * PLANES] + sums[2 * PLANES :] + dot_nn(mix_ref[OWN_AT : OWN_AT + 2 * PLANES], x_lo)
        own[g, 0, :PLANES], own[g, 1, :PLANES] = sums[:PLANES], sums[PLANES:]
        for l in range(LAYERS):
            at, row = FACTOR_ROWS * l, MIX_ROWS * l
            x_hi, x_lo = weighted(at)
            direct = dot_nn(mix_ref[row : row + 8 * WINDOW], x_hi)
            direct = direct[: 4 * WINDOW] + direct[4 * WINDOW :] + dot_nn(mix_ref[row : row + 4 * WINDOW], x_lo)
            x_hi, x_lo = weighted(at + PLANES)
            reflected = dot_nn(mix_ref[row + 8 * WINDOW : row + 12 * WINDOW], x_hi)
            reflected = reflected[: 2 * WINDOW] + reflected[2 * WINDOW :] + dot_nn(mix_ref[row + 8 * WINDOW : row + 10 * WINDOW], x_lo)
            p = start_ref[l]
            q = window_of(p)
            at += 2 * PLANES
            fade, rise, far = (f_ref[g, at + WINDOW * i : at + WINDOW * (i + 1)] for i in range(3))
            for c in (0, 1):
                rows = slice(WINDOW * c, WINDOW * (c + 1))
                near = direct[rows] + own[g, c, pl.ds(q, WINDOW), :]
                after = direct[2 * WINDOW + WINDOW * c : 3 * WINDOW + WINDOW * c]
                sums = near * fade + after * rise + reflected[rows] * far
                kept = mixed[g, c, pl.ds(q, 8), :]
                mixed[g, c, pl.ds(q, 8), :] = jnp.where(plane + q >= p, sums[:8], kept)
                mixed[g, c, pl.ds(pl.multiple_of(q + 8, 8), WINDOW - 8), :] = sums[8:]

    for ky in (0, 1):
        halves = []
        for parity in (0, 1):
            m_hi, m_lo = split(jnp.concatenate([mixed[2 * ky + parity, c, :PLANES] for c in (0, 1)], 0))
            inv = dot3(m_hi, m_lo, t_hi, t_lo)
            halves.append((inv[:PLANES, :HALF] - inv[PLANES:, HALF:], inv[:PLANES, HALF:] + inv[PLANES:, :HALF]))
        even, odd = halves
        turned = (odd[0] * cos - odd[1] * sin, odd[0] * sin + odd[1] * cos)
        for c in (0, 1):
            line[c, ky, :, :HALF] = even[c] + turned[c]
            line[c, ky, :, HALF:] = even[c] - turned[c]
    for group in range(4):
        parts = [line[q // 2, q % 2, :, 128 * group : 128 * (group + 1)] for q in range(4)]
        for i, x in enumerate(exchange(parts)):
            o_ref[:, 4 * group + i] = x.reshape(PLANES // 8, 8, 128)


def inverse_y_kernel(g_ref, contrast_ref, table_ref, tw_ref, o_hbm, o_ref, sems):
    cos, sin = tw_ref[0:1, :], tw_ref[1:2, :]
    t_hi, t_lo = table_ref[: 2 * HALF], table_ref[2 * HALF :]
    copies = []
    planes = contrast_ref.shape[0]
    scale = 1.0 / (4 * HALF * HALF)
    for pair in range(planes // 2):
        both = [jnp.transpose(g_ref[pl.ds(2 * pair + k, HALF, stride=8), :]) for k in (0, 1)]
        m_hi, m_lo = split(jnp.concatenate(both, 0))
        out = dot3(m_hi, m_lo, t_hi, t_lo)
        for k in (0, 1):
            real, imag = out[128 * k : 128 * k + 64], out[128 * k + 64 : 128 * (k + 1)]
            re = real[:, :HALF] - imag[:, HALF:]
            im = real[:, HALF:] + imag[:, :HALF]
            turned = (re[32:] * cos - im[32:] * sin, re[32:] * sin + im[32:] * cos)
            z = 2 * pair + k
            for c, even in enumerate((re[:32], im[:32])):
                o_ref[c, z, :, :HALF] = (even + turned[c]) * (contrast_ref[z, :, :HALF] * scale)
                o_ref[c, z, :, HALF:] = (even - turned[c]) * (contrast_ref[z, :, HALF:] * scale)
        here = pl.ds(2 * pair, 2)
        copies.append(pltpu.make_async_copy(o_ref.at[:, here], o_hbm.at[:, here], sems.at[pair]))
        copies[-1].start()
    for copy in copies:
        copy.wait()


VMEM = pl.BlockSpec(memory_space=pltpu.VMEM)
SMEM = pl.BlockSpec(memory_space=pltpu.SMEM)
HBM = pl.BlockSpec(memory_space=pltpu.HBM)


def call(kernel, out_shape, operands, in_specs, out_specs, flops, scratch=(), limit=16, grid=()):
    operands = [pltpu.with_memory_space_constraint(x, pltpu.HBM) if spec is HBM else x for x, spec in zip(operands, in_specs)]
    return pl.pallas_call(
        kernel,
        grid=grid,
        out_shape=out_shape,
        in_specs=in_specs,
        out_specs=out_specs,
        scratch_shapes=list(scratch),
        compiler_params=pltpu.CompilerParams(vmem_limit_bytes=limit * MIB),
        cost_estimate=pl.CostEstimate(flops=flops, bytes_accessed=4 * MIB, transcendentals=0),
    )(*operands)


def body(wave_field, contrast, layer_of_plane, toeplitz_table, hankel_table, layer_rates):
    table, turn = (jnp.asarray(x) for x in dft_tables())
    ids = jnp.arange(LAYERS, dtype=jnp.int32)
    starts = jnp.sum((layer_of_plane[None, :] < ids[:, None]).astype(jnp.int32), axis=1)
    toeplitz = jnp.pad(toeplitz_table[:, :, ::-1], ((0, 0), (0, 0), (0, 1)))
    hankel = jnp.pad(hankel_table, ((0, 0), (0, 0), (0, 1)))
    ky_pair = (lax.axis_index("lay") * lax.axis_size("lat") + lax.axis_index("lat")).reshape(1)
    planes = contrast.shape[0]
    shape = jax.ShapeDtypeStruct
    dma = pltpu.SemaphoreType.DMA

    sent = call(
        forward_y_kernel,
        shape((2 * HALF * 4, 128), F32),
        (wave_field, table, turn),
        [HBM] * 3,
        HBM,
        6 * 2**27,
        scratch=(
            pltpu.VMEM(wave_field.shape, F32),
            pltpu.VMEM(table.shape, BF16),
            pltpu.VMEM(turn.shape, F32),
            pltpu.VMEM((planes // 2, HALF, HALF), BF16),
            pltpu.VMEM((planes // 2, HALF, HALF), BF16),
            pltpu.VMEM((2 * HALF * 4, 128), F32),
            dma((planes // 2 + 2 + SENDS,)),
        ),
    )
    mix, same_starts = call(
        tables_kernel,
        (pltpu.HBM((OWN_AT + 4 * PLANES, 2 * PLANES), BF16), shape((LAYERS,), jnp.int32)),
        (starts, toeplitz, hankel),
        [SMEM, VMEM, VMEM],
        (pl.BlockSpec((OWN_AT + 4 * PLANES, 2 * PLANES), lambda i: (0, 0)), SMEM),
        2**30,
        grid=(1,),
        scratch=(pltpu.VMEM((4, PLANES + WINDOW, PLANES), F32),),
    )
    factors = call(
        factors_kernel,
        pltpu.HBM((4, ALL_FACTOR_ROWS, HALF), F32),
        (layer_rates, same_starts, ky_pair),
        [SMEM] * 3,
        pl.BlockSpec((1, ALL_FACTOR_ROWS, HALF), lambda g: (g, 0, 0)),
        2**32,
        grid=(4,),
    )
    lines = lax.all_to_all(sent.reshape(HALF, 8, 128), AXES, 0, 0, tiled=True)
    lines = call(
        middle_kernel,
        shape((16, 16, 8, 128), F32),
        (starts, lines.reshape(16, 16, 8, 128), table, turn, mix, factors),
        [SMEM, VMEM, HBM, VMEM, VMEM, HBM],
        VMEM,
        2**32,
        scratch=(
            pltpu.VMEM((2, 2, PLANES, 2 * HALF), F32),
            pltpu.VMEM((4, 2, PLANES, HALF), F32),
            pltpu.VMEM((4, 2, PLANES + WINDOW, HALF), F32),
            pltpu.VMEM((4, 2, PLANES + WINDOW, HALF), F32),
            pltpu.VMEM(factors.shape, F32),
            pltpu.VMEM(table.shape, BF16),
            dma((5,)),
        ),
        limit=24,
    )
    lines = lax.all_to_all(lines.reshape(HALF, 8, 128), AXES, 0, 0, tiled=True)
    return call(
        inverse_y_kernel,
        shape(wave_field.shape, F32),
        (lines.reshape(2 * HALF * 4, 128), contrast, table, turn),
        [VMEM] * 4,
        HBM,
        6 * 2**27,
        scratch=(pltpu.VMEM(wave_field.shape, F32), dma((planes // 2,))),
    )


def solution(mesh):
    return jax.shard_map(
        body,
        mesh=mesh,
        in_specs=(P(None, "lay", "lat", None), P("lay", "lat", None), P(), P(), P(), P()),
        out_specs=P(None, "lay", "lat", None),
        check_vma=False,
    )
```

```python
import math

import jax
import jax.numpy as jnp
import numpy as np
import ml_dtypes
from jax import lax
from jax.experimental import pallas as pl
from jax.experimental.pallas import tpu as pltpu
from jax.sharding import PartitionSpec as P

AXES = ("lay", "lat")
F32 = jnp.float32
BF16 = jnp.bfloat16
HALF = 256
QUARTER = 128
PLANES = 128
LAYERS = 8
WINDOW = 40
MIB = 1 << 20

FACTOR_ROWS = 2 * PLANES + 3 * WINDOW
ALL_FACTOR_ROWS = FACTOR_ROWS * LAYERS + PLANES
MIX_ROWS = 12 * WINDOW
OWN_AT = MIX_ROWS * LAYERS
SENDS = 1


def split_np(x):
    x = x.astype(np.float32)
    hi = x.astype(ml_dtypes.bfloat16)
    lo = (x - hi.astype(np.float32)).astype(ml_dtypes.bfloat16)
    return hi, lo


def dft_tables():
    index = np.arange(QUARTER)
    angle = 2.0 * math.pi / QUARTER * ((index[:, None] * index[None, :]) % QUARTER)
    cos, sin = np.cos(angle), np.sin(angle)
    hi, lo = split_np(np.block([[cos, sin], [-sin, cos]]))
    turn = 2.0 * math.pi / (4 * QUARTER) * np.arange(4)[:, None] * index[None, :]
    return np.concatenate([hi, lo], 0), np.concatenate([np.cos(turn), np.sin(turn)], 0).astype(np.float32)


def split(x):
    hi = x.astype(BF16)
    return hi, (x - hi.astype(F32)).astype(BF16)


def dot_nt(a, b):
    return lax.dot_general(a, b, (((1,), (1,)), ((), ())), preferred_element_type=F32)


def window_of(p):
    return pl.multiple_of((p >> 3) << 3, 8)


def dot_nn(a, b):
    return jnp.dot(a, b, preferred_element_type=F32)


def dot3(dot, a, b):
    return dot(a[0], b[0]) + dot(a[0], b[1]) + dot(a[1], b[0])


def radix_forward(quarters, tw_ref):
    (a_re, a_im), (b_re, b_im), (c_re, c_im), (d_re, d_im) = quarters
    ac_re, ac_im, bd_re, bd_im = a_re + c_re, a_im + c_im, b_re + d_re, b_im + d_im
    am_re, am_im, bm_re, bm_im = a_re - c_re, a_im - c_im, b_re - d_re, b_im - d_im
    out = [
        (ac_re + bd_re, ac_im + bd_im),
        (am_re + bm_im, am_im - bm_re),
        (ac_re - bd_re, ac_im - bd_im),
        (am_re - bm_im, am_im + bm_re),
    ]
    for r in range(1, 4):
        cos, sin = tw_ref[r : r + 1, :], tw_ref[4 + r : 5 + r, :]
        re, im = out[r]
        out[r] = (re * cos + im * sin, im * cos - re * sin)
    return out


def radix_inverse(residues, tw_ref):
    turned = [residues[0]]
    for r in range(1, 4):
        cos, sin = tw_ref[r : r + 1, :], tw_ref[4 + r : 5 + r, :]
        re, im = residues[r]
        turned.append((re * cos - im * sin, re * sin + im * cos))
    (a_re, a_im), (b_re, b_im), (c_re, c_im), (d_re, d_im) = turned
    ac_re, ac_im, bd_re, bd_im = a_re + c_re, a_im + c_im, b_re + d_re, b_im + d_im
    am_re, am_im, bm_re, bm_im = a_re - c_re, a_im - c_im, b_re - d_re, b_im - d_im
    return [
        (ac_re + bd_re, ac_im + bd_im),
        (am_re - bm_im, am_im + bm_re),
        (ac_re - bd_re, ac_im - bd_im),
        (am_re + bm_im, am_im - bm_re),
    ]


def quarter(h):
    return slice(QUARTER * h, QUARTER * (h + 1))


def forward_y_kernel(w_hbm, table_hbm, tw_hbm, o_hbm, w_ref, table_ref, tw_ref, v_hi, v_lo, o_ref, sems):
    pairs = w_ref.shape[1] // 2
    copies = [
        pltpu.make_async_copy(w_hbm.at[:, pl.ds(2 * i, 2)], w_ref.at[:, pl.ds(2 * i, 2)], sems.at[i]) for i in range(pairs)
    ]
    fetch_tw = pltpu.make_async_copy(tw_hbm, tw_ref, sems.at[pairs])
    fetch_table = pltpu.make_async_copy(table_hbm, table_ref, sems.at[pairs + 1])
    for copy in (fetch_tw, copies[0], fetch_table, *copies[1:]):
        copy.start()
    fetch_tw.wait()
    for pair in range(pairs):
        copies[pair].wait()
        rows = []
        for z in (2 * pair, 2 * pair + 1):
            quarters = [[w_ref[c, z, :, quarter(h)] for c in (0, 1)] for h in range(4)]
            rows += [jnp.concatenate(x, 1) for x in radix_forward(quarters, tw_ref)]
        v_hi[pair], v_lo[pair] = split(jnp.concatenate(rows, 0))
    fetch_table.wait()
    count = QUARTER // SENDS
    lane = lax.broadcasted_iota(jnp.int32, (count, 128), 1)
    sends = []
    for part in range(SENDS):
        at = count * part
        table = [
            jnp.concatenate([table_ref[low + at : low + at + count], table_ref[low + QUARTER + at : low + QUARTER + at + count]], 0)
            for low in (0, HALF)
        ]
        for pair in range(pairs):
            out = dot3(dot_nt, table, (v_hi[pair], v_lo[pair]))
            for k in (0, 1):
                re, im = out[:count, 128 * k : 128 * (k + 1)], out[count:, 128 * k : 128 * (k + 1)]
                swapped = pltpu.roll(jnp.where(lane < 64, im, re), 64, 1)
                first = 16 * at + 2 * pair + k
                o_ref[pl.ds(first, count, stride=16), :] = jnp.where(lane < 64, re, swapped)
                o_ref[pl.ds(first + 8, count, stride=16), :] = jnp.where(lane < 64, swapped, im)
        here = pl.ds(16 * at, 16 * count)
        sends.append(pltpu.make_async_copy(o_ref.at[here], o_hbm.at[here], sems.at[pairs + 2 + part]))
        sends[-1].start()
    for send in sends:
        send.wait()


def tables_kernel(start_ref, toe_ref, han_ref, mix_ref, same_start_ref, plane_rows):
    row = lax.broadcasted_iota(jnp.int32, (PLANES, 2 * PLANES), 0)

    def spread(ref, c, amount):
        x = jnp.zeros((PLANES, 2 * PLANES), F32)
        for l in range(LAYERS):
            x = jnp.where(row >= start_ref[l], ref[c, l : l + 1, :], x)
        for bit in range(7):
            moved = pltpu.roll(x, 2 * PLANES - (1 << bit), 1)
            x = jnp.where(((amount >> bit) & 1) == 1, moved, x)
        return x[:, :PLANES]

    def blocks(re, im):
        return jnp.concatenate([jnp.concatenate([re, -im], 1), jnp.concatenate([im, re], 1)], 0)

    plane_rows[:, PLANES:] = jnp.zeros((4, WINDOW, PLANES), F32)
    for c in (0, 1):
        plane_rows[c, :PLANES] = spread(toe_ref, c, PLANES - 1 - row)
        plane_rows[2 + c, :PLANES] = spread(han_ref, c, row)
    z = lax.broadcasted_iota(jnp.int32, (PLANES, PLANES), 0)
    s = lax.broadcasted_iota(jnp.int32, (PLANES, PLANES), 1)
    first = jnp.zeros((PLANES, PLANES), jnp.int32)
    for l in range(LAYERS):
        first = jnp.where(z >= start_ref[l], start_ref[l], first)
    inside = (s >= first) & (s <= z)
    hi, lo = split(blocks(*(jnp.where(inside, plane_rows[c, :PLANES], 0.0) for c in (0, 1))))
    mix_ref[OWN_AT : OWN_AT + 2 * PLANES], mix_ref[OWN_AT + 2 * PLANES :] = hi, lo
    j = lax.broadcasted_iota(jnp.int32, (WINDOW, PLANES), 0)
    s = lax.broadcasted_iota(jnp.int32, (WINDOW, PLANES), 1)
    for l in range(LAYERS):
        p = start_ref[l]
        q = window_of(p)
        re, im, hre, him = (plane_rows[i, pl.ds(q, WINDOW), :] for i in range(4))
        later = jnp.maximum(q + j, p - 1)
        before = blocks(jnp.where(s < p, re, 0.0), jnp.where(s < p, im, 0.0))
        after = blocks(jnp.where(s > later, re, 0.0), jnp.where(s > later, im, 0.0))
        hi, lo = split(jnp.concatenate([before, after], 0))
        at = MIX_ROWS * l
        mix_ref[at : at + 4 * WINDOW], mix_ref[at + 4 * WINDOW : at + 8 * WINDOW] = hi, lo
        mix_ref[at + 8 * WINDOW : at + 10 * WINDOW], mix_ref[at + 10 * WINDOW : at + 12 * WINDOW] = split(blocks(hre, him))
        same_start_ref[l] = p


def factors_kernel(rates_ref, start_ref, ky_ref, f_ref):
    g = pl.program_id(0)

    def signed(k):
        return jnp.where(k >= HALF, k - 2 * HALF, k).astype(F32) / HALF

    lane = lax.broadcasted_iota(jnp.int32, (1, HALF), 1)
    kx = 4 * (lane & (QUARTER - 1)) + 2 * (g % 2) + (lane >> 7)
    freq_y = signed(jnp.full((1, HALF), 2 * ky_ref[0] + g // 2, jnp.int32))
    steep = jnp.sqrt(1.0 + signed(kx) ** 2 + freq_y**2)
    plane = lax.broadcasted_iota(jnp.int32, (PLANES, HALF), 0).astype(F32)
    window = lax.broadcasted_iota(jnp.int32, (WINDOW, HALF), 0).astype(F32)
    own_depth = jnp.zeros((PLANES, HALF), F32)
    for l in range(LAYERS):
        depth = start_ref[l].astype(F32)
        rate = rates_ref[l] / PLANES
        own_depth = jnp.where(plane >= depth, (plane - depth) * rate, own_depth)
        fall = rate * steep
        at = FACTOR_ROWS * l
        f_ref[0, at : at + PLANES] = jnp.exp(-jnp.abs(plane - depth) * fall)
        f_ref[0, at + PLANES : at + 2 * PLANES] = jnp.exp(plane * (-0.5 * fall))
        there = window + window_of(start_ref[l]).astype(F32)
        at += 2 * PLANES
        f_ref[0, at : at + WINDOW] = jnp.exp((depth - there) * fall)
        f_ref[0, at + WINDOW : at + 2 * WINDOW] = jnp.exp((there - depth) * fall)
        f_ref[0, at + 2 * WINDOW : at + 3 * WINDOW] = jnp.exp(there * (-0.5 * fall))
    f_ref[0, FACTOR_ROWS * LAYERS :] = jnp.exp(own_depth * steep)


def exchange(parts):
    piece = lax.broadcasted_iota(jnp.int32, parts[0].shape, 1) // 32
    turned = [x if i == 0 else pltpu.roll(x, 32 * i, 1) for i, x in enumerate(parts)]
    out = []
    for q in range(4):
        x = turned[(3 - q) % 4]
        for p in range(3):
            x = jnp.where(piece == p, turned[(p - q) % 4], x)
        out.append(x if q == 0 else pltpu.roll(x, 128 - 32 * q, 1))
    return out


def middle_kernel(
    start_ref,
    g_ref,
    table_hbm,
    tw_ref,
    mix_ref,
    f_hbm,
    o_ref,
    line,
    spec,
    own,
    mixed,
    f_ref,
    table_ref,
    sems,
):
    fetch_table = pltpu.make_async_copy(table_hbm, table_ref, sems.at[4])
    fetch_table.start()
    for g in range(4):
        pltpu.make_async_copy(f_hbm.at[g], f_ref.at[g], sems.at[g]).start()
    for group in range(4):
        parts = [g_ref[:, 4 * group + i].reshape(PLANES, 128) for i in range(4)]
        for q, x in enumerate(exchange(parts)):
            line[q // 2, q % 2, :, 128 * group : 128 * (group + 1)] = x
    fetch_table.wait()
    table = (table_ref[:HALF], table_ref[HALF:])
    for ky in (0, 1):
        quarters = [[line[c, ky, :, quarter(h)] for c in (0, 1)] for h in range(4)]
        x = jnp.concatenate([jnp.concatenate(v, 1) for v in radix_forward(quarters, tw_ref)], 0)
        out = dot3(dot_nt, split(x), table)
        for r in range(4):
            for c in (0, 1):
                spec[2 * ky + r // 2, c, :, quarter(r % 2)] = out[quarter(r), quarter(c)]

    own[:, :, PLANES:] = jnp.zeros((4, 2, WINDOW, HALF), F32)
    plane = lax.broadcasted_iota(jnp.int32, (8, HALF), 0)

    @pl.loop(0, 4)
    def _(g):
        pltpu.make_async_copy(f_hbm.at[g], f_ref.at[g], sems.at[g]).wait()

        def weighted(at):
            factor = f_ref[g, at : at + PLANES]
            return split(jnp.concatenate([spec[g, 0] * factor, spec[g, 1] * factor], 0))

        x_hi, x_lo = weighted(FACTOR_ROWS * LAYERS)
        sums = dot_nn(mix_ref[OWN_AT:], x_hi)
        sums = sums[: 2 * PLANES] + sums[2 * PLANES :] + dot_nn(mix_ref[OWN_AT : OWN_AT + 2 * PLANES], x_lo)
        own[g, 0, :PLANES], own[g, 1, :PLANES] = sums[:PLANES], sums[PLANES:]
        for l in range(LAYERS):
            at, row = FACTOR_ROWS * l, MIX_ROWS * l
            x_hi, x_lo = weighted(at)
            direct = dot_nn(mix_ref[row : row + 8 * WINDOW], x_hi)
            direct = direct[: 4 * WINDOW] + direct[4 * WINDOW :] + dot_nn(mix_ref[row : row + 4 * WINDOW], x_lo)
            x_hi, x_lo = weighted(at + PLANES)
            reflected = dot_nn(mix_ref[row + 8 * WINDOW : row + 12 * WINDOW], x_hi)
            reflected = reflected[: 2 * WINDOW] + reflected[2 * WINDOW :] + dot_nn(mix_ref[row + 8 * WINDOW : row + 10 * WINDOW], x_lo)
            p = start_ref[l]
            q = window_of(p)
            at += 2 * PLANES
            fade, rise, far = (f_ref[g, at + WINDOW * i : at + WINDOW * (i + 1)] for i in range(3))
            for c in (0, 1):
                rows = slice(WINDOW * c, WINDOW * (c + 1))
                near = direct[rows] + own[g, c, pl.ds(q, WINDOW), :]
                after = direct[2 * WINDOW + WINDOW * c : 3 * WINDOW + WINDOW * c]
                sums = near * fade + after * rise + reflected[rows] * far
                kept = mixed[g, c, pl.ds(q, 8), :]
                mixed[g, c, pl.ds(q, 8), :] = jnp.where(plane + q >= p, sums[:8], kept)
                mixed[g, c, pl.ds(pl.multiple_of(q + 8, 8), WINDOW - 8), :] = sums[8:]

    for ky in (0, 1):
        x = jnp.concatenate(
            [
                jnp.concatenate([mixed[2 * ky + r // 2, c, :PLANES, quarter(r % 2)] for c in (0, 1)], 1)
                for r in range(4)
            ],
            0,
        )
        out = dot3(dot_nn, split(x), table)
        residues = [[out[quarter(r), quarter(c)] for c in (0, 1)] for r in range(4)]
        for h, x in enumerate(radix_inverse(residues, tw_ref)):
            for c in (0, 1):
                line[c, ky, :, quarter(h)] = x[c]
    for group in range(4):
        parts = [line[q // 2, q % 2, :, 128 * group : 128 * (group + 1)] for q in range(4)]
        for i, x in enumerate(exchange(parts)):
            o_ref[:, 4 * group + i] = x.reshape(PLANES // 8, 8, 128)


def inverse_y_kernel(g_ref, contrast_ref, table_ref, tw_ref, o_hbm, o_ref, sems):
    table = (table_ref[:HALF], table_ref[HALF:])
    copies = []
    planes = contrast_ref.shape[0]
    scale = 1.0 / (4 * HALF * HALF)
    for pair in range(planes // 2):
        rows = []
        for z in (2 * pair, 2 * pair + 1):
            for high in (0, 1):
                x = jnp.transpose(g_ref[pl.ds(8 * high + z, QUARTER, stride=16), :])
                rows.append(jnp.concatenate([x[:64], x[64:]], 1))
        out = dot3(dot_nn, split(jnp.concatenate(rows, 0)), table)
        for k in (0, 1):
            z = 2 * pair + k
            at = 128 * k
            residues = [[out[at + 32 * r : at + 32 * (r + 1), quarter(c)] for c in (0, 1)] for r in range(4)]
            for h, x in enumerate(radix_inverse(residues, tw_ref)):
                weight = contrast_ref[z, :, quarter(h)] * scale
                for c in (0, 1):
                    o_ref[c, z, :, quarter(h)] = x[c] * weight
        here = pl.ds(2 * pair, 2)
        copies.append(pltpu.make_async_copy(o_ref.at[:, here], o_hbm.at[:, here], sems.at[pair]))
        copies[-1].start()
    for copy in copies:
        copy.wait()


VMEM = pl.BlockSpec(memory_space=pltpu.VMEM)
SMEM = pl.BlockSpec(memory_space=pltpu.SMEM)
HBM = pl.BlockSpec(memory_space=pltpu.HBM)


def call(kernel, out_shape, operands, in_specs, out_specs, flops, scratch=(), limit=16, grid=()):
    operands = [pltpu.with_memory_space_constraint(x, pltpu.HBM) if spec is HBM else x for x, spec in zip(operands, in_specs)]
    return pl.pallas_call(
        kernel,
        grid=grid,
        out_shape=out_shape,
        in_specs=in_specs,
        out_specs=out_specs,
        scratch_shapes=list(scratch),
        compiler_params=pltpu.CompilerParams(vmem_limit_bytes=limit * MIB),
        cost_estimate=pl.CostEstimate(flops=flops, bytes_accessed=4 * MIB, transcendentals=0),
    )(*operands)


def body(wave_field, contrast, layer_of_plane, toeplitz_table, hankel_table, layer_rates):
    table, turn = (jnp.asarray(x) for x in dft_tables())
    ids = jnp.arange(LAYERS, dtype=jnp.int32)
    starts = jnp.sum((layer_of_plane[None, :] < ids[:, None]).astype(jnp.int32), axis=1)
    toeplitz = jnp.pad(toeplitz_table[:, :, ::-1], ((0, 0), (0, 0), (0, 1)))
    hankel = jnp.pad(hankel_table, ((0, 0), (0, 0), (0, 1)))
    ky_pair = (lax.axis_index("lay") * lax.axis_size("lat") + lax.axis_index("lat")).reshape(1)
    planes = contrast.shape[0]
    shape = jax.ShapeDtypeStruct
    dma = pltpu.SemaphoreType.DMA

    sent = call(
        forward_y_kernel,
        shape((2 * HALF * 4, 128), F32),
        (wave_field, table, turn),
        [HBM] * 3,
        HBM,
        6 * 2**27,
        scratch=(
            pltpu.VMEM(wave_field.shape, F32),
            pltpu.VMEM(table.shape, BF16),
            pltpu.VMEM(turn.shape, F32),
            pltpu.VMEM((planes // 2, HALF, HALF), BF16),
            pltpu.VMEM((planes // 2, HALF, HALF), BF16),
            pltpu.VMEM((2 * HALF * 4, 128), F32),
            dma((planes // 2 + 2 + SENDS,)),
        ),
    )
    mix, same_starts = call(
        tables_kernel,
        (pltpu.HBM((OWN_AT + 4 * PLANES, 2 * PLANES), BF16), shape((LAYERS,), jnp.int32)),
        (starts, toeplitz, hankel),
        [SMEM, VMEM, VMEM],
        (pl.BlockSpec((OWN_AT + 4 * PLANES, 2 * PLANES), lambda i: (0, 0)), SMEM),
        2**30,
        grid=(1,),
        scratch=(pltpu.VMEM((4, PLANES + WINDOW, PLANES), F32),),
    )
    factors = call(
        factors_kernel,
        pltpu.HBM((4, ALL_FACTOR_ROWS, HALF), F32),
        (layer_rates, same_starts, ky_pair),
        [SMEM] * 3,
        pl.BlockSpec((1, ALL_FACTOR_ROWS, HALF), lambda g: (g, 0, 0)),
        2**32,
        grid=(4,),
    )
    lines = lax.all_to_all(sent.reshape(HALF, 8, 128), AXES, 0, 0, tiled=True)
    lines = call(
        middle_kernel,
        shape((16, 16, 8, 128), F32),
        (starts, lines.reshape(16, 16, 8, 128), table, turn, mix, factors),
        [SMEM, VMEM, HBM, VMEM, VMEM, HBM],
        VMEM,
        2**32,
        scratch=(
            pltpu.VMEM((2, 2, PLANES, 2 * HALF), F32),
            pltpu.VMEM((4, 2, PLANES, HALF), F32),
            pltpu.VMEM((4, 2, PLANES + WINDOW, HALF), F32),
            pltpu.VMEM((4, 2, PLANES + WINDOW, HALF), F32),
            pltpu.VMEM(factors.shape, F32),
            pltpu.VMEM(table.shape, BF16),
            dma((5,)),
        ),
        limit=24,
    )
    lines = lax.all_to_all(lines.reshape(HALF, 8, 128), AXES, 0, 0, tiled=True)
    return call(
        inverse_y_kernel,
        shape(wave_field.shape, F32),
        (lines.reshape(2 * HALF * 4, 128), contrast, table, turn),
        [VMEM] * 4,
        HBM,
        6 * 2**27,
        scratch=(pltpu.VMEM(wave_field.shape, F32), dma((planes // 2,))),
    )


def solution(mesh):
    return jax.shard_map(
        body,
        mesh=mesh,
        in_specs=(P(None, "lay", "lat", None), P("lay", "lat", None), P(), P(), P(), P()),
        out_specs=P(None, "lay", "lat", None),
        check_vma=False,
    )
```

```python
import math

import jax
import jax.numpy as jnp
import numpy as np
import ml_dtypes
from jax import lax
from jax.experimental import pallas as pl
from jax.experimental.pallas import tpu as pltpu
from jax.sharding import PartitionSpec as P

AXES = ("lay", "lat")
F32 = jnp.float32
BF16 = jnp.bfloat16
HALF = 256
QUARTER = 128
PLANES = 128
LAYERS = 8
WINDOW = 40
MIB = 1 << 20

FACTOR_ROWS = 2 * PLANES + 3 * WINDOW
ALL_FACTOR_ROWS = FACTOR_ROWS * LAYERS
MIX_ROWS = 12 * WINDOW
OWN_AT = MIX_ROWS * LAYERS
SENDS = 1


def split_np(x):
    x = x.astype(np.float32)
    hi = x.astype(ml_dtypes.bfloat16)
    lo = (x - hi.astype(np.float32)).astype(ml_dtypes.bfloat16)
    return hi, lo


def dft_tables():
    index = np.arange(QUARTER)
    angle = 2.0 * math.pi / QUARTER * ((index[:, None] * index[None, :]) % QUARTER)
    cos, sin = np.cos(angle), np.sin(angle)
    hi, lo = split_np(np.block([[cos, sin], [-sin, cos]]))
    turn = 2.0 * math.pi / (4 * QUARTER) * np.arange(4)[:, None] * index[None, :]
    return np.concatenate([hi, lo], 0), np.concatenate([np.cos(turn), np.sin(turn)], 0).astype(np.float32)


def split(x):
    hi = x.astype(BF16)
    return hi, (x - hi.astype(F32)).astype(BF16)


def dot_nt(a, b):
    return lax.dot_general(a, b, (((1,), (1,)), ((), ())), preferred_element_type=F32)


def window_of(p):
    return pl.multiple_of((p >> 3) << 3, 8)


def dot_nn(a, b):
    return jnp.dot(a, b, preferred_element_type=F32)


def dot3(dot, a, b):
    return dot(a[0], b[0]) + dot(a[0], b[1]) + dot(a[1], b[0])


def radix_forward(quarters, tw_ref):
    (a_re, a_im), (b_re, b_im), (c_re, c_im), (d_re, d_im) = quarters
    ac_re, ac_im, bd_re, bd_im = a_re + c_re, a_im + c_im, b_re + d_re, b_im + d_im
    am_re, am_im, bm_re, bm_im = a_re - c_re, a_im - c_im, b_re - d_re, b_im - d_im
    out = [
        (ac_re + bd_re, ac_im + bd_im),
        (am_re + bm_im, am_im - bm_re),
        (ac_re - bd_re, ac_im - bd_im),
        (am_re - bm_im, am_im + bm_re),
    ]
    for r in range(1, 4):
        cos, sin = tw_ref[r : r + 1, :], tw_ref[4 + r : 5 + r, :]
        re, im = out[r]
        out[r] = (re * cos + im * sin, im * cos - re * sin)
    return out


def radix_inverse(residues, tw_ref):
    turned = [residues[0]]
    for r in range(1, 4):
        cos, sin = tw_ref[r : r + 1, :], tw_ref[4 + r : 5 + r, :]
        re, im = residues[r]
        turned.append((re * cos - im * sin, re * sin + im * cos))
    (a_re, a_im), (b_re, b_im), (c_re, c_im), (d_re, d_im) = turned
    ac_re, ac_im, bd_re, bd_im = a_re + c_re, a_im + c_im, b_re + d_re, b_im + d_im
    am_re, am_im, bm_re, bm_im = a_re - c_re, a_im - c_im, b_re - d_re, b_im - d_im
    return [
        (ac_re + bd_re, ac_im + bd_im),
        (am_re - bm_im, am_im + bm_re),
        (ac_re - bd_re, ac_im - bd_im),
        (am_re + bm_im, am_im - bm_re),
    ]


def quarter(h):
    return slice(QUARTER * h, QUARTER * (h + 1))


def forward_y_kernel(w_hbm, table_hbm, tw_hbm, o_hbm, w_ref, table_ref, tw_ref, v_hi, v_lo, o_ref, sems):
    pairs = w_ref.shape[1] // 2
    copies = [
        pltpu.make_async_copy(w_hbm.at[:, pl.ds(2 * i, 2)], w_ref.at[:, pl.ds(2 * i, 2)], sems.at[i]) for i in range(pairs)
    ]
    fetch_tw = pltpu.make_async_copy(tw_hbm, tw_ref, sems.at[pairs])
    fetch_table = pltpu.make_async_copy(table_hbm, table_ref, sems.at[pairs + 1])
    for copy in (fetch_tw, copies[0], fetch_table, *copies[1:]):
        copy.start()
    fetch_tw.wait()
    for pair in range(pairs):
        copies[pair].wait()
        rows = []
        for z in (2 * pair, 2 * pair + 1):
            quarters = [[w_ref[c, z, :, quarter(h)] for c in (0, 1)] for h in range(4)]
            rows += [jnp.concatenate(x, 1) for x in radix_forward(quarters, tw_ref)]
        v_hi[pair], v_lo[pair] = split(jnp.concatenate(rows, 0))
    fetch_table.wait()
    count = QUARTER // SENDS
    lane = lax.broadcasted_iota(jnp.int32, (count, 128), 1)
    sends = []
    for part in range(SENDS):
        at = count * part
        table = [
            jnp.concatenate([table_ref[low + at : low + at + count], table_ref[low + QUARTER + at : low + QUARTER + at + count]], 0)
            for low in (0, HALF)
        ]
        for pair in range(pairs):
            out = dot3(dot_nt, table, (v_hi[pair], v_lo[pair]))
            for k in (0, 1):
                re, im = out[:count, 128 * k : 128 * (k + 1)], out[count:, 128 * k : 128 * (k + 1)]
                swapped = pltpu.roll(jnp.where(lane < 64, im, re), 64, 1)
                first = 16 * at + 2 * pair + k
                o_ref[pl.ds(first, count, stride=16), :] = jnp.where(lane < 64, re, swapped)
                o_ref[pl.ds(first + 8, count, stride=16), :] = jnp.where(lane < 64, swapped, im)
        here = pl.ds(16 * at, 16 * count)
        sends.append(pltpu.make_async_copy(o_ref.at[here], o_hbm.at[here], sems.at[pairs + 2 + part]))
        sends[-1].start()
    for send in sends:
        send.wait()


def tables_kernel(start_ref, toe_ref, han_ref, mix_ref, same_start_ref, plane_rows):
    row = lax.broadcasted_iota(jnp.int32, (PLANES, 2 * PLANES), 0)

    def spread(ref, c, amount):
        x = jnp.zeros((PLANES, 2 * PLANES), F32)
        for l in range(LAYERS):
            x = jnp.where(row >= start_ref[l], ref[c, l : l + 1, :], x)
        for bit in range(7):
            moved = pltpu.roll(x, 2 * PLANES - (1 << bit), 1)
            x = jnp.where(((amount >> bit) & 1) == 1, moved, x)
        return x[:, :PLANES]

    def blocks(re, im):
        return jnp.concatenate([jnp.concatenate([re, -im], 1), jnp.concatenate([im, re], 1)], 0)

    plane_rows[:, PLANES:] = jnp.zeros((4, WINDOW, PLANES), F32)
    for c in (0, 1):
        plane_rows[c, :PLANES] = spread(toe_ref, c, PLANES - 1 - row)
        plane_rows[2 + c, :PLANES] = spread(han_ref, c, row)
    z = lax.broadcasted_iota(jnp.int32, (PLANES, PLANES), 0)
    s = lax.broadcasted_iota(jnp.int32, (PLANES, PLANES), 1)
    first = jnp.zeros((PLANES, PLANES), jnp.int32)
    for l in range(LAYERS):
        first = jnp.where(z >= start_ref[l], start_ref[l], first)
    inside = (s >= first) & (s <= z)
    hi, lo = split(blocks(*(jnp.where(inside, plane_rows[c, :PLANES], 0.0) for c in (0, 1))))
    mix_ref[OWN_AT : OWN_AT + 2 * PLANES], mix_ref[OWN_AT + 2 * PLANES :] = hi, lo
    j = lax.broadcasted_iota(jnp.int32, (WINDOW, PLANES), 0)
    s = lax.broadcasted_iota(jnp.int32, (WINDOW, PLANES), 1)
    for l in range(LAYERS):
        p = start_ref[l]
        q = window_of(p)
        re, im, hre, him = (plane_rows[i, pl.ds(q, WINDOW), :] for i in range(4))
        later = jnp.maximum(q + j, p - 1)
        before = blocks(jnp.where(s < p, re, 0.0), jnp.where(s < p, im, 0.0))
        after = blocks(jnp.where(s > later, re, 0.0), jnp.where(s > later, im, 0.0))
        hi, lo = split(jnp.concatenate([before, after], 0))
        at = MIX_ROWS * l
        mix_ref[at : at + 4 * WINDOW], mix_ref[at + 4 * WINDOW : at + 8 * WINDOW] = hi, lo
        mix_ref[at + 8 * WINDOW : at + 10 * WINDOW], mix_ref[at + 10 * WINDOW : at + 12 * WINDOW] = split(blocks(hre, him))
        same_start_ref[l] = p


def factors_kernel(rates_ref, start_ref, ky_ref, f_ref, own_f_ref):
    g = pl.program_id(0)

    def signed(k):
        return jnp.where(k >= HALF, k - 2 * HALF, k).astype(F32) / HALF

    lane = lax.broadcasted_iota(jnp.int32, (1, HALF), 1)
    kx = 4 * (lane & (QUARTER - 1)) + 2 * (g % 2) + (lane >> 7)
    freq_y = signed(jnp.full((1, HALF), 2 * ky_ref[0] + g // 2, jnp.int32))
    steep = jnp.sqrt(1.0 + signed(kx) ** 2 + freq_y**2)
    plane = lax.broadcasted_iota(jnp.int32, (PLANES, HALF), 0).astype(F32)
    window = lax.broadcasted_iota(jnp.int32, (WINDOW, HALF), 0).astype(F32)
    own_depth = jnp.zeros((PLANES, HALF), F32)
    for l in range(LAYERS):
        depth = start_ref[l].astype(F32)
        rate = rates_ref[l] / PLANES
        own_depth = jnp.where(plane >= depth, (plane - depth) * rate, own_depth)
        fall = rate * steep
        at = FACTOR_ROWS * l
        f_ref[0, at : at + PLANES] = jnp.exp(-jnp.abs(plane - depth) * fall)
        f_ref[0, at + PLANES : at + 2 * PLANES] = jnp.exp(plane * (-0.5 * fall))
        there = window + window_of(start_ref[l]).astype(F32)
        at += 2 * PLANES
        f_ref[0, at : at + WINDOW] = jnp.exp((depth - there) * fall)
        f_ref[0, at + WINDOW : at + 2 * WINDOW] = jnp.exp((there - depth) * fall)
        f_ref[0, at + 2 * WINDOW : at + 3 * WINDOW] = jnp.exp(there * (-0.5 * fall))
    own_f_ref[0] = jnp.exp(own_depth * steep)


def exchange(parts):
    piece = lax.broadcasted_iota(jnp.int32, parts[0].shape, 1) // 32
    turned = [x if i == 0 else pltpu.roll(x, 32 * i, 1) for i, x in enumerate(parts)]
    out = []
    for q in range(4):
        x = turned[(3 - q) % 4]
        for p in range(3):
            x = jnp.where(piece == p, turned[(p - q) % 4], x)
        out.append(x if q == 0 else pltpu.roll(x, 128 - 32 * q, 1))
    return out


def middle_kernel(
    start_ref,
    g_ref,
    table_hbm,
    tw_ref,
    mix_ref,
    f_hbm,
    own_f_hbm,
    o_ref,
    line,
    spec,
    own,
    mixed,
    f_ref,
    own_f_ref,
    table_ref,
    sems,
):
    fetch_table = pltpu.make_async_copy(table_hbm, table_ref, sems.at[4])
    fetch_table.start()
    fetch_own = pltpu.make_async_copy(own_f_hbm, own_f_ref, sems.at[5])
    fetch_own.start()
    for g in range(4):
        pltpu.make_async_copy(f_hbm.at[g], f_ref.at[g], sems.at[g]).start()
    for group in range(4):
        parts = [g_ref[:, 4 * group + i].reshape(PLANES, 128) for i in range(4)]
        for q, x in enumerate(exchange(parts)):
            line[q // 2, q % 2, :, 128 * group : 128 * (group + 1)] = x
    fetch_table.wait()
    table = (table_ref[:HALF], table_ref[HALF:])
    for ky in (0, 1):
        quarters = [[line[c, ky, :, quarter(h)] for c in (0, 1)] for h in range(4)]
        x = jnp.concatenate([jnp.concatenate(v, 1) for v in radix_forward(quarters, tw_ref)], 0)
        out = dot3(dot_nt, split(x), table)
        for r in range(4):
            for c in (0, 1):
                spec[2 * ky + r // 2, c, :, quarter(r % 2)] = out[quarter(r), quarter(c)]

    own[:, :, PLANES:] = jnp.zeros((4, 2, WINDOW, HALF), F32)
    plane = lax.broadcasted_iota(jnp.int32, (8, HALF), 0)
    fetch_own.wait()
    for g in range(4):
        x_hi, x_lo = split(jnp.concatenate([spec[g, 0] * own_f_ref[g], spec[g, 1] * own_f_ref[g]], 0))
        sums = dot_nn(mix_ref[OWN_AT:], x_hi)
        sums = sums[: 2 * PLANES] + sums[2 * PLANES :] + dot_nn(mix_ref[OWN_AT : OWN_AT + 2 * PLANES], x_lo)
        own[g, 0, :PLANES], own[g, 1, :PLANES] = sums[:PLANES], sums[PLANES:]

    @pl.loop(0, 4)
    def _(g):
        pltpu.make_async_copy(f_hbm.at[g], f_ref.at[g], sems.at[g]).wait()

        def weighted(at):
            factor = f_ref[g, at : at + PLANES]
            return split(jnp.concatenate([spec[g, 0] * factor, spec[g, 1] * factor], 0))

        for l in range(LAYERS):
            at, row = FACTOR_ROWS * l, MIX_ROWS * l
            x_hi, x_lo = weighted(at)
            direct = dot_nn(mix_ref[row : row + 8 * WINDOW], x_hi)
            direct = direct[: 4 * WINDOW] + direct[4 * WINDOW :] + dot_nn(mix_ref[row : row + 4 * WINDOW], x_lo)
            x_hi, x_lo = weighted(at + PLANES)
            reflected = dot_nn(mix_ref[row + 8 * WINDOW : row + 12 * WINDOW], x_hi)
            reflected = reflected[: 2 * WINDOW] + reflected[2 * WINDOW :] + dot_nn(mix_ref[row + 8 * WINDOW : row + 10 * WINDOW], x_lo)
            p = start_ref[l]
            q = window_of(p)
            at += 2 * PLANES
            fade, rise, far = (f_ref[g, at + WINDOW * i : at + WINDOW * (i + 1)] for i in range(3))
            for c in (0, 1):
                rows = slice(WINDOW * c, WINDOW * (c + 1))
                near = direct[rows] + own[g, c, pl.ds(q, WINDOW), :]
                after = direct[2 * WINDOW + WINDOW * c : 3 * WINDOW + WINDOW * c]
                sums = near * fade + after * rise + reflected[rows] * far
                kept = mixed[g, c, pl.ds(q, 8), :]
                mixed[g, c, pl.ds(q, 8), :] = jnp.where(plane + q >= p, sums[:8], kept)
                mixed[g, c, pl.ds(pl.multiple_of(q + 8, 8), WINDOW - 8), :] = sums[8:]

    for ky in (0, 1):
        x = jnp.concatenate(
            [
                jnp.concatenate([mixed[2 * ky + r // 2, c, :PLANES, quarter(r % 2)] for c in (0, 1)], 1)
                for r in range(4)
            ],
            0,
        )
        out = dot3(dot_nn, split(x), table)
        residues = [[out[quarter(r), quarter(c)] for c in (0, 1)] for r in range(4)]
        for h, x in enumerate(radix_inverse(residues, tw_ref)):
            for c in (0, 1):
                line[c, ky, :, quarter(h)] = x[c]
    for group in range(4):
        parts = [line[q // 2, q % 2, :, 128 * group : 128 * (group + 1)] for q in range(4)]
        for i, x in enumerate(exchange(parts)):
            o_ref[:, 4 * group + i] = x.reshape(PLANES // 8, 8, 128)


def inverse_y_kernel(g_ref, contrast_ref, table_ref, tw_ref, o_hbm, o_ref, sems):
    table = (table_ref[:HALF], table_ref[HALF:])
    copies = []
    planes = contrast_ref.shape[0]
    scale = 1.0 / (4 * HALF * HALF)
    for pair in range(planes // 2):
        rows = []
        for z in (2 * pair, 2 * pair + 1):
            for high in (0, 1):
                x = jnp.transpose(g_ref[pl.ds(8 * high + z, QUARTER, stride=16), :])
                rows.append(jnp.concatenate([x[:64], x[64:]], 1))
        out = dot3(dot_nn, split(jnp.concatenate(rows, 0)), table)
        for k in (0, 1):
            z = 2 * pair + k
            at = 128 * k
            residues = [[out[at + 32 * r : at + 32 * (r + 1), quarter(c)] for c in (0, 1)] for r in range(4)]
            for h, x in enumerate(radix_inverse(residues, tw_ref)):
                weight = contrast_ref[z, :, quarter(h)] * scale
                for c in (0, 1):
                    o_ref[c, z, :, quarter(h)] = x[c] * weight
        here = pl.ds(2 * pair, 2)
        copies.append(pltpu.make_async_copy(o_ref.at[:, here], o_hbm.at[:, here], sems.at[pair]))
        copies[-1].start()
    for copy in copies:
        copy.wait()


VMEM = pl.BlockSpec(memory_space=pltpu.VMEM)
SMEM = pl.BlockSpec(memory_space=pltpu.SMEM)
HBM = pl.BlockSpec(memory_space=pltpu.HBM)


def call(kernel, out_shape, operands, in_specs, out_specs, flops, scratch=(), limit=16, grid=()):
    operands = [pltpu.with_memory_space_constraint(x, pltpu.HBM) if spec is HBM else x for x, spec in zip(operands, in_specs)]
    return pl.pallas_call(
        kernel,
        grid=grid,
        out_shape=out_shape,
        in_specs=in_specs,
        out_specs=out_specs,
        scratch_shapes=list(scratch),
        compiler_params=pltpu.CompilerParams(vmem_limit_bytes=limit * MIB),
        cost_estimate=pl.CostEstimate(flops=flops, bytes_accessed=4 * MIB, transcendentals=0),
    )(*operands)


def body(wave_field, contrast, layer_of_plane, toeplitz_table, hankel_table, layer_rates):
    table, turn = (jnp.asarray(x) for x in dft_tables())
    ids = jnp.arange(LAYERS, dtype=jnp.int32)
    starts = jnp.sum((layer_of_plane[None, :] < ids[:, None]).astype(jnp.int32), axis=1)
    toeplitz = jnp.pad(toeplitz_table[:, :, ::-1], ((0, 0), (0, 0), (0, 1)))
    hankel = jnp.pad(hankel_table, ((0, 0), (0, 0), (0, 1)))
    ky_pair = (lax.axis_index("lay") * lax.axis_size("lat") + lax.axis_index("lat")).reshape(1)
    planes = contrast.shape[0]
    shape = jax.ShapeDtypeStruct
    dma = pltpu.SemaphoreType.DMA

    sent = call(
        forward_y_kernel,
        shape((2 * HALF * 4, 128), F32),
        (wave_field, table, turn),
        [HBM] * 3,
        HBM,
        6 * 2**27,
        scratch=(
            pltpu.VMEM(wave_field.shape, F32),
            pltpu.VMEM(table.shape, BF16),
            pltpu.VMEM(turn.shape, F32),
            pltpu.VMEM((planes // 2, HALF, HALF), BF16),
            pltpu.VMEM((planes // 2, HALF, HALF), BF16),
            pltpu.VMEM((2 * HALF * 4, 128), F32),
            dma((planes // 2 + 2 + SENDS,)),
        ),
    )
    mix, same_starts = call(
        tables_kernel,
        (pltpu.HBM((OWN_AT + 4 * PLANES, 2 * PLANES), BF16), shape((LAYERS,), jnp.int32)),
        (starts, toeplitz, hankel),
        [SMEM, VMEM, VMEM],
        (pl.BlockSpec((OWN_AT + 4 * PLANES, 2 * PLANES), lambda i: (0, 0)), SMEM),
        2**30,
        grid=(1,),
        scratch=(pltpu.VMEM((4, PLANES + WINDOW, PLANES), F32),),
    )
    factors, own_factors = call(
        factors_kernel,
        (pltpu.HBM((4, ALL_FACTOR_ROWS, HALF), F32), pltpu.HBM((4, PLANES, HALF), F32)),
        (layer_rates, same_starts, ky_pair),
        [SMEM] * 3,
        (
            pl.BlockSpec((1, ALL_FACTOR_ROWS, HALF), lambda g: (g, 0, 0)),
            pl.BlockSpec((1, PLANES, HALF), lambda g: (g, 0, 0)),
        ),
        2**32,
        grid=(4,),
    )
    lines = lax.all_to_all(sent.reshape(HALF, 8, 128), AXES, 0, 0, tiled=True)
    lines = call(
        middle_kernel,
        shape((16, 16, 8, 128), F32),
        (starts, lines.reshape(16, 16, 8, 128), table, turn, mix, factors, own_factors),
        [SMEM, VMEM, HBM, VMEM, VMEM, HBM, HBM],
        VMEM,
        2**32,
        scratch=(
            pltpu.VMEM((2, 2, PLANES, 2 * HALF), F32),
            pltpu.VMEM((4, 2, PLANES, HALF), F32),
            pltpu.VMEM((4, 2, PLANES + WINDOW, HALF), F32),
            pltpu.VMEM((4, 2, PLANES + WINDOW, HALF), F32),
            pltpu.VMEM(factors.shape, F32),
            pltpu.VMEM(own_factors.shape, F32),
            pltpu.VMEM(table.shape, BF16),
            dma((6,)),
        ),
        limit=24,
    )
    lines = lax.all_to_all(lines.reshape(HALF, 8, 128), AXES, 0, 0, tiled=True)
    return call(
        inverse_y_kernel,
        shape(wave_field.shape, F32),
        (lines.reshape(2 * HALF * 4, 128), contrast, table, turn),
        [VMEM] * 4,
        HBM,
        6 * 2**27,
        scratch=(pltpu.VMEM(wave_field.shape, F32), dma((planes // 2,))),
    )


def solution(mesh):
    return jax.shard_map(
        body,
        mesh=mesh,
        in_specs=(P(None, "lay", "lat", None), P("lay", "lat", None), P(), P(), P(), P()),
        out_specs=P(None, "lay", "lat", None),
        check_vma=False,
    )
```

```python
import math

import jax
import jax.numpy as jnp
import numpy as np
import ml_dtypes
from jax import lax
from jax.experimental import pallas as pl
from jax.experimental.pallas import tpu as pltpu
from jax.sharding import PartitionSpec as P

AXES = ("lay", "lat")
F32 = jnp.float32
BF16 = jnp.bfloat16
HALF = 256
QUARTER = 128
PLANES = 128
LAYERS = 8
WINDOW = 40
MIB = 1 << 20

FACTOR_ROWS = 2 * PLANES + 3 * WINDOW
ALL_FACTOR_ROWS = FACTOR_ROWS * LAYERS
MIX_ROWS = 12 * WINDOW
OWN_AT = MIX_ROWS * LAYERS
SENDS = 1


def split_np(x):
    x = x.astype(np.float32)
    hi = x.astype(ml_dtypes.bfloat16)
    lo = (x - hi.astype(np.float32)).astype(ml_dtypes.bfloat16)
    return hi, lo


def dft_tables():
    index = np.arange(QUARTER)
    angle = 2.0 * math.pi / QUARTER * ((index[:, None] * index[None, :]) % QUARTER)
    cos, sin = np.cos(angle), np.sin(angle)
    hi, lo = split_np(np.block([[cos, sin], [-sin, cos]]))
    turn = 2.0 * math.pi / (4 * QUARTER) * np.arange(4)[:, None] * index[None, :]
    return np.concatenate([hi, lo], 0), np.concatenate([np.cos(turn), np.sin(turn)], 0).astype(np.float32)


def split(x):
    hi = x.astype(BF16)
    return hi, (x - hi.astype(F32)).astype(BF16)


def dot_nt(a, b):
    return lax.dot_general(a, b, (((1,), (1,)), ((), ())), preferred_element_type=F32)


def window_of(p):
    return pl.multiple_of((p >> 3) << 3, 8)


def dot_nn(a, b):
    return jnp.dot(a, b, preferred_element_type=F32)


def dot3(dot, a, b):
    return dot(a[0], b[0]) + dot(a[0], b[1]) + dot(a[1], b[0])


def radix_forward(quarters, tw_ref):
    (a_re, a_im), (b_re, b_im), (c_re, c_im), (d_re, d_im) = quarters
    ac_re, ac_im, bd_re, bd_im = a_re + c_re, a_im + c_im, b_re + d_re, b_im + d_im
    am_re, am_im, bm_re, bm_im = a_re - c_re, a_im - c_im, b_re - d_re, b_im - d_im
    out = [
        (ac_re + bd_re, ac_im + bd_im),
        (am_re + bm_im, am_im - bm_re),
        (ac_re - bd_re, ac_im - bd_im),
        (am_re - bm_im, am_im + bm_re),
    ]
    for r in range(1, 4):
        cos, sin = tw_ref[r : r + 1, :], tw_ref[4 + r : 5 + r, :]
        re, im = out[r]
        out[r] = (re * cos + im * sin, im * cos - re * sin)
    return out


def radix_inverse(residues, tw_ref):
    turned = [residues[0]]
    for r in range(1, 4):
        cos, sin = tw_ref[r : r + 1, :], tw_ref[4 + r : 5 + r, :]
        re, im = residues[r]
        turned.append((re * cos - im * sin, re * sin + im * cos))
    (a_re, a_im), (b_re, b_im), (c_re, c_im), (d_re, d_im) = turned
    ac_re, ac_im, bd_re, bd_im = a_re + c_re, a_im + c_im, b_re + d_re, b_im + d_im
    am_re, am_im, bm_re, bm_im = a_re - c_re, a_im - c_im, b_re - d_re, b_im - d_im
    return [
        (ac_re + bd_re, ac_im + bd_im),
        (am_re - bm_im, am_im + bm_re),
        (ac_re - bd_re, ac_im - bd_im),
        (am_re + bm_im, am_im - bm_re),
    ]


def quarter(h):
    return slice(QUARTER * h, QUARTER * (h + 1))


def forward_y_kernel(w_hbm, table_hbm, tw_hbm, o_hbm, w_ref, table_ref, tw_ref, v_hi, v_lo, o_ref, sems):
    pairs = w_ref.shape[1] // 2
    copies = [
        pltpu.make_async_copy(w_hbm.at[:, pl.ds(2 * i, 2)], w_ref.at[:, pl.ds(2 * i, 2)], sems.at[i]) for i in range(pairs)
    ]
    fetch_tw = pltpu.make_async_copy(tw_hbm, tw_ref, sems.at[pairs])
    fetch_table = pltpu.make_async_copy(table_hbm, table_ref, sems.at[pairs + 1])
    for copy in (fetch_tw, copies[0], fetch_table, *copies[1:]):
        copy.start()
    fetch_tw.wait()
    for pair in range(pairs):
        copies[pair].wait()
        rows = []
        for z in (2 * pair, 2 * pair + 1):
            quarters = [[w_ref[c, z, :, quarter(h)] for c in (0, 1)] for h in range(4)]
            rows += [jnp.concatenate(x, 1) for x in radix_forward(quarters, tw_ref)]
        v_hi[pair], v_lo[pair] = split(jnp.concatenate(rows, 0))
    fetch_table.wait()
    count = QUARTER // SENDS
    lane = lax.broadcasted_iota(jnp.int32, (count, 128), 1)
    sends = []
    for part in range(SENDS):
        at = count * part
        table = [
            jnp.concatenate([table_ref[low + at : low + at + count], table_ref[low + QUARTER + at : low + QUARTER + at + count]], 0)
            for low in (0, HALF)
        ]
        for pair in range(pairs):
            out = dot3(dot_nt, table, (v_hi[pair], v_lo[pair]))
            for k in (0, 1):
                re, im = out[:count, 128 * k : 128 * (k + 1)], out[count:, 128 * k : 128 * (k + 1)]
                swapped = pltpu.roll(jnp.where(lane < 64, im, re), 64, 1)
                first = 16 * at + 2 * pair + k
                o_ref[pl.ds(first, count, stride=16), :] = jnp.where(lane < 64, re, swapped)
                o_ref[pl.ds(first + 8, count, stride=16), :] = jnp.where(lane < 64, swapped, im)
        here = pl.ds(16 * at, 16 * count)
        sends.append(pltpu.make_async_copy(o_ref.at[here], o_hbm.at[here], sems.at[pairs + 2 + part]))
        sends[-1].start()
    for send in sends:
        send.wait()


def tables_kernel(start_ref, toe_ref, han_ref, mix_ref, same_start_ref, plane_rows):
    row = lax.broadcasted_iota(jnp.int32, (PLANES, 2 * PLANES), 0)

    def spread(ref, c, amount):
        x = jnp.zeros((PLANES, 2 * PLANES), F32)
        for l in range(LAYERS):
            x = jnp.where(row >= start_ref[l], ref[c, l : l + 1, :], x)
        for bit in range(7):
            moved = pltpu.roll(x, 2 * PLANES - (1 << bit), 1)
            x = jnp.where(((amount >> bit) & 1) == 1, moved, x)
        return x[:, :PLANES]

    def blocks(re, im):
        return jnp.concatenate([jnp.concatenate([re, -im], 1), jnp.concatenate([im, re], 1)], 0)

    plane_rows[:, PLANES:] = jnp.zeros((4, WINDOW, PLANES), F32)
    for c in (0, 1):
        plane_rows[c, :PLANES] = spread(toe_ref, c, PLANES - 1 - row)
        plane_rows[2 + c, :PLANES] = spread(han_ref, c, row)
    z = lax.broadcasted_iota(jnp.int32, (PLANES, PLANES), 0)
    s = lax.broadcasted_iota(jnp.int32, (PLANES, PLANES), 1)
    first = jnp.zeros((PLANES, PLANES), jnp.int32)
    for l in range(LAYERS):
        first = jnp.where(z >= start_ref[l], start_ref[l], first)
    inside = (s >= first) & (s <= z)
    hi, lo = split(blocks(*(jnp.where(inside, plane_rows[c, :PLANES], 0.0) for c in (0, 1))))
    mix_ref[OWN_AT : OWN_AT + 2 * PLANES], mix_ref[OWN_AT + 2 * PLANES :] = hi, lo
    j = lax.broadcasted_iota(jnp.int32, (WINDOW, PLANES), 0)
    s = lax.broadcasted_iota(jnp.int32, (WINDOW, PLANES), 1)
    for l in range(LAYERS):
        p = start_ref[l]
        q = window_of(p)
        re, im, hre, him = (plane_rows[i, pl.ds(q, WINDOW), :] for i in range(4))
        later = jnp.maximum(q + j, p - 1)
        before = blocks(jnp.where(s < p, re, 0.0), jnp.where(s < p, im, 0.0))
        after = blocks(jnp.where(s > later, re, 0.0), jnp.where(s > later, im, 0.0))
        hi, lo = split(jnp.concatenate([before, after], 0))
        at = MIX_ROWS * l
        mix_ref[at : at + 4 * WINDOW], mix_ref[at + 4 * WINDOW : at + 8 * WINDOW] = hi, lo
        mix_ref[at + 8 * WINDOW : at + 10 * WINDOW], mix_ref[at + 10 * WINDOW : at + 12 * WINDOW] = split(blocks(hre, him))
        same_start_ref[l] = p


def factors_kernel(rates_ref, start_ref, ky_ref, f_ref, own_f_ref):
    g = pl.program_id(0)

    def signed(k):
        return jnp.where(k >= HALF, k - 2 * HALF, k).astype(F32) / HALF

    lane = lax.broadcasted_iota(jnp.int32, (1, HALF), 1)
    kx = 4 * (lane & (QUARTER - 1)) + 2 * (g % 2) + (lane >> 7)
    freq_y = signed(jnp.full((1, HALF), 2 * ky_ref[0] + g // 2, jnp.int32))
    steep = jnp.sqrt(1.0 + signed(kx) ** 2 + freq_y**2)
    plane = lax.broadcasted_iota(jnp.int32, (PLANES, HALF), 0).astype(F32)
    window = lax.broadcasted_iota(jnp.int32, (WINDOW, HALF), 0).astype(F32)
    own_depth = jnp.zeros((PLANES, HALF), F32)
    for l in range(LAYERS):
        depth = start_ref[l].astype(F32)
        rate = rates_ref[l] / PLANES
        own_depth = jnp.where(plane >= depth, (plane - depth) * rate, own_depth)
        fall = rate * steep
        at = FACTOR_ROWS * l
        f_ref[0, at : at + PLANES] = jnp.exp(-jnp.abs(plane - depth) * fall)
        f_ref[0, at + PLANES : at + 2 * PLANES] = jnp.exp(plane * (-0.5 * fall))
        there = window + window_of(start_ref[l]).astype(F32)
        at += 2 * PLANES
        f_ref[0, at : at + WINDOW] = jnp.exp((depth - there) * fall)
        f_ref[0, at + WINDOW : at + 2 * WINDOW] = jnp.exp((there - depth) * fall)
        f_ref[0, at + 2 * WINDOW : at + 3 * WINDOW] = jnp.exp(there * (-0.5 * fall))
    own_f_ref[0] = jnp.exp(own_depth * steep)


def exchange(parts):
    piece = lax.broadcasted_iota(jnp.int32, parts[0].shape, 1) // 32
    turned = [x if i == 0 else pltpu.roll(x, 32 * i, 1) for i, x in enumerate(parts)]
    out = []
    for q in range(4):
        x = turned[(3 - q) % 4]
        for p in range(3):
            x = jnp.where(piece == p, turned[(p - q) % 4], x)
        out.append(x if q == 0 else pltpu.roll(x, 128 - 32 * q, 1))
    return out


def middle_kernel(
    start_ref,
    g_ref,
    table_hbm,
    tw_ref,
    mix_ref,
    f_hbm,
    own_f_hbm,
    o_ref,
    line,
    spec,
    own,
    mixed,
    f_ref,
    own_f_ref,
    table_ref,
    sems,
):
    fetch_table = pltpu.make_async_copy(table_hbm, table_ref, sems.at[4])
    fetch_table.start()
    fetch_own = pltpu.make_async_copy(own_f_hbm, own_f_ref, sems.at[5])
    fetch_own.start()
    for g in range(4):
        pltpu.make_async_copy(f_hbm.at[g], f_ref.at[g], sems.at[g]).start()
    for group in range(4):
        parts = [g_ref[:, 4 * group + i].reshape(PLANES, 128) for i in range(4)]
        for q, x in enumerate(exchange(parts)):
            line[q // 2, q % 2, :, 128 * group : 128 * (group + 1)] = x
    fetch_table.wait()
    table = (table_ref[:HALF], table_ref[HALF:])
    for ky in (0, 1):
        quarters = [[line[c, ky, :, quarter(h)] for c in (0, 1)] for h in range(4)]
        x = jnp.concatenate([jnp.concatenate(v, 1) for v in radix_forward(quarters, tw_ref)], 0)
        out = dot3(dot_nt, split(x), table)
        for r in range(4):
            for c in (0, 1):
                spec[2 * ky + r // 2, c, :, quarter(r % 2)] = out[quarter(r), quarter(c)]

    own[:, :, PLANES:] = jnp.zeros((4, 2, WINDOW, HALF), F32)
    plane = lax.broadcasted_iota(jnp.int32, (8, HALF), 0)
    fetch_own.wait()
    for g in range(4):
        x_hi, x_lo = split(jnp.concatenate([spec[g, 0] * own_f_ref[g], spec[g, 1] * own_f_ref[g]], 0))
        sums = dot_nn(mix_ref[OWN_AT:], x_hi)
        sums = sums[: 2 * PLANES] + sums[2 * PLANES :] + dot_nn(mix_ref[OWN_AT : OWN_AT + 2 * PLANES], x_lo)
        own[g, 0, :PLANES], own[g, 1, :PLANES] = sums[:PLANES], sums[PLANES:]

    @pl.loop(0, 4, unroll=2)
    def _(g):
        pltpu.make_async_copy(f_hbm.at[g], f_ref.at[g], sems.at[g]).wait()

        def weighted(at):
            factor = f_ref[g, at : at + PLANES]
            return split(jnp.concatenate([spec[g, 0] * factor, spec[g, 1] * factor], 0))

        for l in range(LAYERS):
            at, row = FACTOR_ROWS * l, MIX_ROWS * l
            x_hi, x_lo = weighted(at)
            direct = dot_nn(mix_ref[row : row + 8 * WINDOW], x_hi)
            direct = direct[: 4 * WINDOW] + direct[4 * WINDOW :] + dot_nn(mix_ref[row : row + 4 * WINDOW], x_lo)
            x_hi, x_lo = weighted(at + PLANES)
            reflected = dot_nn(mix_ref[row + 8 * WINDOW : row + 12 * WINDOW], x_hi)
            reflected = reflected[: 2 * WINDOW] + reflected[2 * WINDOW :] + dot_nn(mix_ref[row + 8 * WINDOW : row + 10 * WINDOW], x_lo)
            p = start_ref[l]
            q = window_of(p)
            at += 2 * PLANES
            fade, rise, far = (f_ref[g, at + WINDOW * i : at + WINDOW * (i + 1)] for i in range(3))
            for c in (0, 1):
                rows = slice(WINDOW * c, WINDOW * (c + 1))
                near = direct[rows] + own[g, c, pl.ds(q, WINDOW), :]
                after = direct[2 * WINDOW + WINDOW * c : 3 * WINDOW + WINDOW * c]
                sums = near * fade + after * rise + reflected[rows] * far
                kept = mixed[g, c, pl.ds(q, 8), :]
                mixed[g, c, pl.ds(q, 8), :] = jnp.where(plane + q >= p, sums[:8], kept)
                mixed[g, c, pl.ds(pl.multiple_of(q + 8, 8), WINDOW - 8), :] = sums[8:]

    for ky in (0, 1):
        x = jnp.concatenate(
            [
                jnp.concatenate([mixed[2 * ky + r // 2, c, :PLANES, quarter(r % 2)] for c in (0, 1)], 1)
                for r in range(4)
            ],
            0,
        )
        out = dot3(dot_nn, split(x), table)
        residues = [[out[quarter(r), quarter(c)] for c in (0, 1)] for r in range(4)]
        for h, x in enumerate(radix_inverse(residues, tw_ref)):
            for c in (0, 1):
                line[c, ky, :, quarter(h)] = x[c]
    for group in range(4):
        parts = [line[q // 2, q % 2, :, 128 * group : 128 * (group + 1)] for q in range(4)]
        for i, x in enumerate(exchange(parts)):
            o_ref[:, 4 * group + i] = x.reshape(PLANES // 8, 8, 128)


def inverse_y_kernel(g_ref, contrast_ref, table_ref, tw_ref, o_hbm, o_ref, sems):
    table = (table_ref[:HALF], table_ref[HALF:])
    copies = []
    planes = contrast_ref.shape[0]
    scale = 1.0 / (4 * HALF * HALF)
    for pair in range(planes // 2):
        rows = []
        for z in (2 * pair, 2 * pair + 1):
            for high in (0, 1):
                x = jnp.transpose(g_ref[pl.ds(8 * high + z, QUARTER, stride=16), :])
                rows.append(jnp.concatenate([x[:64], x[64:]], 1))
        out = dot3(dot_nn, split(jnp.concatenate(rows, 0)), table)
        for k in (0, 1):
            z = 2 * pair + k
            at = 128 * k
            residues = [[out[at + 32 * r : at + 32 * (r + 1), quarter(c)] for c in (0, 1)] for r in range(4)]
            for h, x in enumerate(radix_inverse(residues, tw_ref)):
                weight = contrast_ref[z, :, quarter(h)] * scale
                for c in (0, 1):
                    o_ref[c, z, :, quarter(h)] = x[c] * weight
        here = pl.ds(2 * pair, 2)
        copies.append(pltpu.make_async_copy(o_ref.at[:, here], o_hbm.at[:, here], sems.at[pair]))
        copies[-1].start()
    for copy in copies:
        copy.wait()


VMEM = pl.BlockSpec(memory_space=pltpu.VMEM)
SMEM = pl.BlockSpec(memory_space=pltpu.SMEM)
HBM = pl.BlockSpec(memory_space=pltpu.HBM)


def call(kernel, out_shape, operands, in_specs, out_specs, flops, scratch=(), limit=16, grid=()):
    operands = [pltpu.with_memory_space_constraint(x, pltpu.HBM) if spec is HBM else x for x, spec in zip(operands, in_specs)]
    return pl.pallas_call(
        kernel,
        grid=grid,
        out_shape=out_shape,
        in_specs=in_specs,
        out_specs=out_specs,
        scratch_shapes=list(scratch),
        compiler_params=pltpu.CompilerParams(vmem_limit_bytes=limit * MIB),
        cost_estimate=pl.CostEstimate(flops=flops, bytes_accessed=4 * MIB, transcendentals=0),
    )(*operands)


def body(wave_field, contrast, layer_of_plane, toeplitz_table, hankel_table, layer_rates):
    table, turn = (jnp.asarray(x) for x in dft_tables())
    ids = jnp.arange(LAYERS, dtype=jnp.int32)
    starts = jnp.sum((layer_of_plane[None, :] < ids[:, None]).astype(jnp.int32), axis=1)
    toeplitz = jnp.pad(toeplitz_table[:, :, ::-1], ((0, 0), (0, 0), (0, 1)))
    hankel = jnp.pad(hankel_table, ((0, 0), (0, 0), (0, 1)))
    ky_pair = (lax.axis_index("lay") * lax.axis_size("lat") + lax.axis_index("lat")).reshape(1)
    planes = contrast.shape[0]
    shape = jax.ShapeDtypeStruct
    dma = pltpu.SemaphoreType.DMA

    sent = call(
        forward_y_kernel,
        shape((2 * HALF * 4, 128), F32),
        (wave_field, table, turn),
        [HBM] * 3,
        HBM,
        6 * 2**27,
        scratch=(
            pltpu.VMEM(wave_field.shape, F32),
            pltpu.VMEM(table.shape, BF16),
            pltpu.VMEM(turn.shape, F32),
            pltpu.VMEM((planes // 2, HALF, HALF), BF16),
            pltpu.VMEM((planes // 2, HALF, HALF), BF16),
            pltpu.VMEM((2 * HALF * 4, 128), F32),
            dma((planes // 2 + 2 + SENDS,)),
        ),
    )
    mix, same_starts = call(
        tables_kernel,
        (pltpu.HBM((OWN_AT + 4 * PLANES, 2 * PLANES), BF16), shape((LAYERS,), jnp.int32)),
        (starts, toeplitz, hankel),
        [SMEM, VMEM, VMEM],
        (pl.BlockSpec((OWN_AT + 4 * PLANES, 2 * PLANES), lambda i: (0, 0)), SMEM),
        2**30,
        grid=(1,),
        scratch=(pltpu.VMEM((4, PLANES + WINDOW, PLANES), F32),),
    )
    factors, own_factors = call(
        factors_kernel,
        (pltpu.HBM((4, ALL_FACTOR_ROWS, HALF), F32), pltpu.HBM((4, PLANES, HALF), F32)),
        (layer_rates, same_starts, ky_pair),
        [SMEM] * 3,
        (
            pl.BlockSpec((1, ALL_FACTOR_ROWS, HALF), lambda g: (g, 0, 0)),
            pl.BlockSpec((1, PLANES, HALF), lambda g: (g, 0, 0)),
        ),
        2**32,
        grid=(4,),
    )
    lines = lax.all_to_all(sent.reshape(HALF, 8, 128), AXES, 0, 0, tiled=True)
    lines = call(
        middle_kernel,
        shape((16, 16, 8, 128), F32),
        (starts, lines.reshape(16, 16, 8, 128), table, turn, mix, factors, own_factors),
        [SMEM, VMEM, HBM, VMEM, VMEM, HBM, HBM],
        VMEM,
        2**32,
        scratch=(
            pltpu.VMEM((2, 2, PLANES, 2 * HALF), F32),
            pltpu.VMEM((4, 2, PLANES, HALF), F32),
            pltpu.VMEM((4, 2, PLANES + WINDOW, HALF), F32),
            pltpu.VMEM((4, 2, PLANES + WINDOW, HALF), F32),
            pltpu.VMEM(factors.shape, F32),
            pltpu.VMEM(own_factors.shape, F32),
            pltpu.VMEM(table.shape, BF16),
            dma((6,)),
        ),
        limit=24,
    )
    lines = lax.all_to_all(lines.reshape(HALF, 8, 128), AXES, 0, 0, tiled=True)
    return call(
        inverse_y_kernel,
        shape(wave_field.shape, F32),
        (lines.reshape(2 * HALF * 4, 128), contrast, table, turn),
        [VMEM] * 4,
        HBM,
        6 * 2**27,
        scratch=(pltpu.VMEM(wave_field.shape, F32), dma((planes // 2,))),
    )


def solution(mesh):
    return jax.shard_map(
        body,
        mesh=mesh,
        in_specs=(P(None, "lay", "lat", None), P("lay", "lat", None), P(), P(), P(), P()),
        out_specs=P(None, "lay", "lat", None),
        check_vma=False,
    )
```
